256 devices in a mesh: node: 32 (over z, x), local: 8 (over y, core).
Axes of the slice: x: 4, y: 4, z: 8, core: 2. Of those that a mesh axis runs over, the one named last changes fastest.
Arguments:
- pooled_grad: bfloat16 [131072, 128], P(('node', 'local')), may hold values from -40 to 40, as said below
- lengths: int32 [131072], P(('node', 'local')), may hold values from 1 to 32
- slot_of: int32 [131072, 32], P(('node', 'local')), may hold values from 0 to 16383, as said below
- slot_row: int32 [524288], P(('node', 'local')), may hold values from 0 to 1048575, as said below
- table: float32 [1048576, 128], P(('node', 'local')), may hold values from -6 to 6
- accum: float32 [1048576], P(('node', 'local')), may hold values from 0.05 to 2
Outputs:
- table_new: float32 [1048576, 128], P(('node', 'local'))
- accum_new: float32 [1048576], P(('node', 'local'))
The draws below stay inside these ranges and needn't reach their ends.
Inputs may be any that keep to these rules, and one draw needn't show every extreme that they name: `pooled_grad`: spread over rows and columns. `slot_row`: slot u of node m's table, u = l * 2048 + n * 64 + c with c < 64, holds a row of device n * 8 + l (rows d * 4096 to (d + 1) * 4096 - 1 belong to device d); this group of 64 slots is the bucket (m, l, n). Ids name only the first live slots of each bucket; bucket (m, l, (m + 1) % 32) has all 64 live, every other bucket one to 32 live, and bucket (m, l, (m + 2) % 32) exactly 32. An id position of a sample of node m names slot slot_of of node m's table.
All inputs are finite; a program needn't handle non-finite values.
Results may differ from the reference program's by a relative error of at most 0.0003.
Values may be sent and summed in bfloat16 or wider, within the bound.
No kernel may reach another device: no remote copies, remote signals or barrier semaphores. Data moves between devices by JAX's collectives and lax.ppermute only.
A program may use at most 64 MiB of HBM per device.

```python
import math
import jax
import jax.numpy as jnp
from jax import lax

E = 128
POOL = 32
SAMP_DEV = 512
CAP = 64
ROWS_DEV = 4096
SAMPLES = 131072
NODE_SLOTS = 16384
ALL_SLOTS = 524288
ROWS = 1048576
N_NODE = 32
N_LOCAL = 8


def slot_layout(key):
    key_live, key_base = jax.random.split(key, 2)
    live_count = jax.random.randint(key_live, (N_NODE, N_LOCAL, N_NODE), (CAP + 2) // 3, CAP // 2 + 1)
    source = jnp.arange(N_NODE)[:, None, None]
    target = jnp.arange(N_NODE)[None, None, :]
    filled = target == (source + 1) % N_NODE
    halfway = target == (source + 2) % N_NODE
    live_count = jnp.where(halfway, CAP // 2, live_count)
    live_count = jnp.where(filled, CAP, live_count)
    base_row = jax.random.randint(key_base, (N_NODE, N_LOCAL, N_NODE), 0, 64)
    return (live_count, base_row)


def draw_pooled_grad(key, part):
    key = jax.random.fold_in(key, 11)
    key_base, key_rows, key_cols = jax.random.split(key, 3)
    row_scale = jnp.exp(jax.random.uniform(key_rows, (SAMPLES, 1), jnp.float32, 0.0, 2.3))
    col_scale = jnp.exp(jax.random.uniform(key_cols, (1, E), jnp.float32, 0.0, 2.3))
    values = jax.random.truncated_normal(key_base, -4.0, 4.0, (SAMPLES, E), jnp.float32)
    return (0.1 * values * row_scale * col_scale).astype(jnp.bfloat16)


def draw_slot_row(key, part):
    live_count, base_row = slot_layout(key)
    key = jax.random.fold_in(key, 21)
    stride = 2 * jax.random.randint(key, (N_NODE, N_LOCAL, N_NODE, 1), 0, 20) + 1
    within = jnp.arange(CAP, dtype=jnp.int32)[None, None, None, :]
    aggregator = jnp.arange(N_LOCAL, dtype=jnp.int32)[None, :, None, None]
    target = jnp.arange(N_NODE, dtype=jnp.int32)[None, None, :, None]
    owner = target * N_LOCAL + aggregator
    local_row = (base_row[:, :, :, None] + stride * within) % ROWS_DEV
    return (owner * ROWS_DEV + local_row).reshape(ALL_SLOTS).astype(jnp.int32)


def draw_slot_of(key, part):
    live_count, base_row = slot_layout(key)
    key = jax.random.fold_in(key, 22)
    key_bucket, key_pick = jax.random.split(key)
    node_of = jnp.arange(SAMPLES, dtype=jnp.int32) // (SAMP_DEV * N_LOCAL)
    bucket = jax.random.randint(key_bucket, (SAMPLES, POOL), 0, N_LOCAL * N_NODE)
    picked = jax.random.randint(key_pick, (SAMPLES, POOL), 0, CAP)
    live_flat = live_count.reshape(N_NODE, N_LOCAL * N_NODE)
    live_here = live_flat[node_of[:, None], bucket]
    return (bucket * CAP + picked % live_here).astype(jnp.int32)


def touch_ends(drawn, stream_key, least, high):
    index_at = [jax.random.randint(jax.random.fold_in(stream_key, axis), (), 0, length) for axis, length in enumerate(drawn.shape)]
    main_axis = drawn.shape.index(max(drawn.shape))
    beside = index_at[:main_axis] + [(index_at[main_axis] + 1) % drawn.shape[main_axis]] + index_at[main_axis + 1:]
    return drawn.at[tuple(index_at)].set(least).at[tuple(beside)].set(high)


def shard_levels(own_key, dims, shards, low, top_value):
    factor_of, own = 1.0, jax.random.fold_in(own_key, 6)
    for position, parts in shards:
        steps = jnp.exp(jax.random.uniform(jax.random.fold_in(own, position), (parts,), jnp.float32, low / len(shards), top_value / len(shards)))
        factor_of = factor_of * jnp.repeat(steps, dims[position] // parts).reshape([-1 if axis == position else 1 for axis in range(len(dims))])
    return factor_of


def noise(own_key, dims, scale, most, pieces=(), kind=jnp.bfloat16):
    result = scale * jax.random.normal(own_key, dims, jnp.float32)
    if pieces:
        result = result * shard_levels(own_key, dims, pieces, -0.22, 0.18)
    return jnp.clip(result, -most, most).astype(kind)


def setup_inputs(seed: int = 0) -> dict:
    splits = jax.random.split(jax.random.key(seed), 7)
    pooled_grad = draw_pooled_grad(jax.random.fold_in(splits[6], 71), 0)
    lengths = touch_ends(jax.random.randint(splits[1], (SAMPLES,), 1, POOL + 1), jax.random.fold_in(splits[1], 1), 1, POOL).astype(jnp.int32)
    slot_of = draw_slot_of(jax.random.fold_in(splits[6], 71), 0)
    slot_row = draw_slot_row(jax.random.fold_in(splits[6], 71), 0)
    table = noise(splits[4], (ROWS, E), 1.0, 6.0, ((0, 256),), jnp.float32)
    accum = jnp.clip(jnp.exp(math.log(2.0) - 3.6888794 * jax.random.uniform(splits[5], (ROWS,), jnp.float32) ** shard_levels(splits[5], (ROWS,), ((0, 256),), -0.2, 0.2)), 0.05, 2.0)
    return dict(pooled_grad=pooled_grad, lengths=lengths, slot_of=slot_of, slot_row=slot_row, table=table, accum=accum)


LEARN_RATE = 0.3
EPSILON = 1e-06

def reference(pooled_grad, lengths, slot_of, slot_row, table, accum):
    node_rows = SAMP_DEV * N_LOCAL
    pooled = pooled_grad.astype(jnp.float32).reshape(N_NODE, node_rows, E)
    slot_ids = slot_of.reshape(N_NODE, node_rows, POOL)
    bag_lens = lengths.reshape(N_NODE, node_rows)
    positions = jnp.arange(POOL, dtype=jnp.int32)
    present = positions[None, None, :] < bag_lens[:, :, None]
    tables = slot_row.reshape(N_NODE, NODE_SLOTS)

    def add_node(running, inputs):
        grads_node, slots_node, present_node, table_node = inputs
        row_id = table_node[slots_node]
        contrib = jnp.where(present_node[:, :, None], grads_node[:, None, :], jnp.zeros((), jnp.float32))
        running = running.at[row_id.reshape(-1)].add(contrib.reshape(-1, E))
        return (running, None)
    gradient, unused = lax.scan(add_node, jnp.zeros((ROWS, E), jnp.float32), (pooled, slot_ids, present, tables))
    accum_new = accum + lax.optimization_barrier(jnp.mean(gradient * gradient, axis=1))
    table_new = table - LEARN_RATE * gradient / (jnp.sqrt(accum_new)[:, None] + EPSILON)
    return (table_new, accum_new)
```

```python
import jax
import jax.numpy as jnp
from jax import lax
from jax.experimental import pallas as pl
from jax.experimental.pallas import tpu as pltpu
from jax.sharding import PartitionSpec as P

LEARN_RATE = 0.3
EPSILON = 1e-06

LANES = 128
KEEP = 32
GROUP = 8
BLOCKS = 17
OWN = 9 * LANES
BUCKET_ROWS = 40
F32, BF16, I32 = jnp.float32, jnp.bfloat16, jnp.int32


def rows_iota(rows, cols):
    return lax.broadcasted_iota(I32, (rows, cols), 0)


def lanes_iota(rows, cols):
    return lax.broadcasted_iota(I32, (rows, cols), 1)


def prep_kernel(slot_ref, len_ref, pooled_ref, out_ref, perm_ref):
    slot = slot_ref[...]
    present = rows_iota(*slot.shape) < len_ref[...]
    side = (slot >> 11) & 1
    owner = (slot >> 6) & 31
    place = slot & 63
    first = place < KEEP
    low = jnp.where(first, (owner & 3) * KEEP + place, side * KEEP + place - KEEP)
    low = jnp.where(present, low, -1)
    block = (slot >> 12) * BLOCKS + jnp.where(first, side * 8 + (owner >> 2), 16)

    def by_group(x):
        parts = [x[:, LANES * b : LANES * (b + 1)] for b in range(4)]
        return jnp.concatenate(parts, axis=0).T.astype(BF16)

    out_ref[512:640, :] = by_group(low.astype(F32))
    out_ref[640:768, :] = by_group(block.astype(F32))
    for h in range(2):
        for b in range(4):
            start = b * 128 + h * 64
            perm_ref[pl.ds(h * 4 + b, 64, stride=GROUP), :] = pooled_ref[start : start + 64, :].astype(F32)
    for t in range(4):
        out_ref[t * 128 : (t + 1) * 128, :] = perm_ref[t * 128 : (t + 1) * 128, :].T.astype(BF16)


def sums_kernel(place_ref, got_ref, own_ref, other_ref, low_ref, code_ref, counts_ref):
    chip, core = place_ref[0], place_ref[1]
    for ch in range(4):
        base = ch * 768
        low_ref[ch * 128 : (ch + 1) * 128, :] = got_ref[base + 512 : base + 640, :].astype(F32)
        block = got_ref[base + 640 : base + 768, :].astype(F32).astype(I32) - chip * BLOCKS
        valid = (block >= 0) & (block < BLOCKS)
        block = jnp.where(block < 16, block ^ (core * 8), block)
        member = (rows_iota(128, 128) >> 6) * 4 + (lanes_iota(128, 128) >> 5)
        code = jnp.where(valid, block * GROUP + member, -1)
        code_ref[ch * 128 : (ch + 1) * 128, :] = code.astype(F32)

    tiles = [(rows_iota(16, 128) + 16 * t).astype(F32).astype(BF16) for t in range(9)]
    one, zero = jnp.ones((16, 128), BF16), jnp.zeros((16, 128), BF16)

    def onehot(ref, row, count):
        halves = []
        for h in range(2):
            line = ref[pl.ds(row + h * 64, 1), :]
            line = jnp.broadcast_to(line, (16, 128)).astype(BF16)
            halves.append(jnp.concatenate([jnp.where(line == tiles[t], one, zero) for t in range(count)], axis=0))
        return jnp.concatenate(halves, axis=1)

    def group_counts(row):
        return lax.dot_general(
            onehot(code_ref, row, 9), onehot(low_ref, row, 8), (((1,), (1,)), ((), ())), preferred_element_type=F32
        )

    def step(i, carry):
        ch, pair = i // 32, i % 32
        row = ch * 128 + pair * 2
        first, second = group_counts(row), group_counts(row + 1)
        at = pl.multiple_of(i * 16, 16)
        for b in range(BLOCKS):
            both = jnp.concatenate([first[b * 8 : b * 8 + 8, :], second[b * 8 : b * 8 + 8, :]], axis=0)
            counts_ref[pl.ds(at, 16), b * 128 : (b + 1) * 128] = both.astype(BF16)
        return carry

    lax.fori_loop(0, 128, step, 0, unroll=4)

    pooled = jnp.concatenate(
        [got_ref[ch * 768 + t * 128 : ch * 768 + (t + 1) * 128, :] for ch in range(4) for t in range(4)], axis=1
    )
    total = jnp.dot(pooled, counts_ref[...], preferred_element_type=F32)
    own_ref[:, :1024] = total[:, :1024]
    other_ref[:, :1024] = total[:, 1024:2048]
    own_ref[:, 1024:] = total[:, 2048:]
    other_ref[:, 1024:] = total[:, 2048:]


def code_kernel(place_ref, own_ref, got_ref, row_ref, out_ref, over_ref):
    core, node = place_ref[1], place_ref[2]
    rows = row_ref[...] & 4095
    next_node = (node + 1) & 31

    def coded(b):
        total = own_ref[:, b * 128 : (b + 1) * 128] + got_ref[:, b * 128 : (b + 1) * 128]
        most = jnp.max(jnp.abs(total), axis=0, keepdims=True)
        power = jnp.floor(jnp.log2(jnp.maximum(most, 1e-30))) + 1.0
        scaled = jnp.clip(jnp.round(total * jnp.exp2(15.0 - power)), -32767.0, 32767.0)
        return scaled.T.astype(I32).astype(jnp.int16), power.astype(I32)

    def tail(row_line, power_line):
        at = rows_iota(8, 128)
        out = jnp.where(at == 0, jnp.broadcast_to(row_line, (8, 128)), jnp.broadcast_to(power_line, (8, 128)))
        return out

    for b in range(8):
        codes, power = coded(b)
        for q in range(4):
            n = b * 4 + q
            out_ref[n, 0:32, :] = codes[q * 32 : (q + 1) * 32, :]
            out_ref[n, 32:40, :] = tail(rows[n >> 1 : (n >> 1) + 1, :], power).astype(jnp.int16)
    codes, power = coded(8)
    over_ref[0:64, :] = codes[0:64, :]
    over_ref[64:72, :] = tail(row_ref[pl.ds(next_node >> 1, 1), :] & 4095, power).astype(jnp.int16)


def update_kernel(place_ref, got_ref, over_ref, table_ref, accum_ref, table_out, accum_out, value_ref, line_ref):
    core, node = place_ref[1], place_ref[2]
    rb = pl.program_id(0)

    @pl.when(rb == 0)
    def _():
        def halves(x):
            x = x.astype(I32)
            return (x >> 8).astype(F32).astype(BF16), (x & 255).astype(F32).astype(BF16)

        for m in range(32):
            high, low = halves(got_ref[m, 0:32, :])
            value_ref[m * 32 : (m + 1) * 32, 0:128] = high
            value_ref[m * 32 : (m + 1) * 32, 128:256] = low
        start = pl.multiple_of(core * 32, 32)
        high, low = halves(over_ref[pl.ds(start, 32), :])
        value_ref[1024:1056, 0:128] = high
        value_ref[1024:1056, 128:256] = low
        value_ref[1056:1152, :] = jnp.zeros((96, 256), BF16)

        quarter = lanes_iota(8, 128) >> 5
        ids, powers = jnp.zeros((8, 128), I32), jnp.zeros((8, 128), I32)
        for r in range(4):
            tails = [got_ref[kb * 4 + r, 32:40, :].astype(I32) for kb in range(8)]
            id_lines = jnp.concatenate([t[0:1, :] for t in tails], axis=0)
            power_lines = jnp.concatenate([t[1:2, :] for t in tails], axis=0)
            id_lines = pltpu.roll(id_lines, (r * 32 + 128 - (node & 1) * 64) & 127, axis=1)
            power_lines = pltpu.roll(power_lines, (r * 32 + 128 - (node & 3) * 32) & 127, axis=1)
            ids = jnp.where(quarter == r, id_lines, ids)
            powers = jnp.where(quarter == r, power_lines, powers)
        line_ref[0:8, :] = ids
        line_ref[8:16, :] = powers
        over_tail = over_ref[64:72, :].astype(I32)
        over_ids = pltpu.roll(over_tail, (128 - ((node & 1) * 64 + 32)) & 127, axis=1)
        over_powers = pltpu.roll(over_tail, (128 - core * 32) & 127, axis=1)
        lane = lanes_iota(1, 128)
        line_ref[16:17, :] = jnp.where(lane < 32, over_ids[0:1, :], -1)
        line_ref[17:18, :] = over_powers[1:2, :]

    tiles = [(rows_iota(16, 128) + 16 * t).astype(F32).astype(BF16) for t in range(16)]
    zero = jnp.zeros((16, 128), BF16)
    parts = []
    for kb in range(9):
        at_id, at_power = (kb, kb + 8) if kb < 8 else (16, 17)
        ids = (line_ref[at_id : at_id + 1, :] - rb * 256).astype(F32)
        ids = jnp.broadcast_to(ids, (16, 128)).astype(BF16)
        scale = jnp.exp2(line_ref[at_power : at_power + 1, :].astype(F32) - 15.0)
        scale = jnp.broadcast_to(scale, (16, 128)).astype(BF16)
        parts.append(jnp.concatenate([jnp.where(ids == tiles[t], scale, zero) for t in range(16)], axis=0))
    hot = jnp.concatenate(parts, axis=1)
    both = jnp.dot(hot, value_ref[...], preferred_element_type=F32)
    gradient = both[:, 0:128] * 256.0 + both[:, 128:256]
    for t in range(2):
        g = gradient[t * 128 : (t + 1) * 128, :]
        diag = rows_iota(128, 128) == lanes_iota(128, 128)
        accum = jnp.broadcast_to(accum_ref[pl.ds(rb * 2 + t, 1), :], (128, 128))
        fresh = jnp.sum(g * g * (1.0 / 128.0) + jnp.where(diag, accum, 0.0), axis=1, keepdims=True)
        accum_out[pl.ds(rb * 2 + t, 1), :] = jnp.sum(jnp.where(diag, fresh, 0.0), axis=0, keepdims=True)
        step = LEARN_RATE * g / (jnp.sqrt(fresh) + EPSILON)
        table_out[t * 128 : (t + 1) * 128, :] = table_ref[t * 128 : (t + 1) * 128, :] - step


VMEM = pl.BlockSpec(memory_space=pltpu.VMEM)
SMEM = pl.BlockSpec(memory_space=pltpu.SMEM)
PARAMS = pltpu.CompilerParams(vmem_limit_bytes=40 * 1024 * 1024)


def prep(slot_t, lengths, pooled):
    return pl.pallas_call(
        prep_kernel,
        out_shape=jax.ShapeDtypeStruct((768, 128), BF16),
        in_specs=[VMEM] * 3,
        out_specs=VMEM,
        scratch_shapes=[pltpu.VMEM((512, 128), F32)],
        compiler_params=PARAMS,
        name="prep",
    )(slot_t, lengths, pooled)


def sums(place, got):
    return pl.pallas_call(
        sums_kernel,
        out_shape=[jax.ShapeDtypeStruct((128, OWN), F32)] * 2,
        in_specs=[SMEM, VMEM],
        out_specs=[VMEM] * 2,
        scratch_shapes=[
            pltpu.VMEM((512, 128), F32),
            pltpu.VMEM((512, 128), F32),
            pltpu.VMEM((2048, BLOCKS * 128), BF16),
        ],
        compiler_params=PARAMS,
        name="sums",
    )(place, got)


def code(place, own, got, slot_row):
    return pl.pallas_call(
        code_kernel,
        out_shape=[
            jax.ShapeDtypeStruct((32, BUCKET_ROWS, 128), jnp.int16),
            jax.ShapeDtypeStruct((80, 128), jnp.int16),
        ],
        in_specs=[SMEM] + [VMEM] * 3,
        out_specs=[VMEM] * 2,
        compiler_params=PARAMS,
        name="code",
    )(place, own, got, slot_row)


def update(place, got, over, table, accum):
    whole = lambda shape: pl.BlockSpec(shape, lambda i: (0,) * len(shape))
    return pl.pallas_call(
        update_kernel,
        grid=(16,),
        out_shape=[jax.ShapeDtypeStruct((4096, 128), F32), jax.ShapeDtypeStruct((32, 128), F32)],
        in_specs=[
            SMEM,
            whole((32, BUCKET_ROWS, 128)),
            whole((80, 128)),
            pl.BlockSpec((256, 128), lambda i: (i, 0)),
            whole((32, 128)),
        ],
        out_specs=[pl.BlockSpec((256, 128), lambda i: (i, 0)), whole((32, 128))],
        scratch_shapes=[pltpu.VMEM((1152, 256), BF16), pltpu.VMEM((24, 128), I32)],
        compiler_params=PARAMS,
        name="update",
    )(place, got, over, table, accum)


def per_device(pooled_grad, lengths, slot_of, slot_row, table, accum):
    local, node = lax.axis_index("local"), lax.axis_index("node")
    place = jnp.stack([local >> 1, local & 1, node]).astype(I32)
    packed = prep(slot_of.T, lengths.reshape(1, 512), pooled_grad)
    same_core = [[0, 2, 4, 6], [1, 3, 5, 7]]
    got = lax.all_gather(packed, "local", axis=0, tiled=True, axis_index_groups=same_core)
    own, other = sums(place, got)
    other = lax.ppermute(other, "local", [(i, i ^ 1) for i in range(8)])
    codes, over = code(place, own, other, slot_row.reshape(16, 128))
    over = lax.ppermute(over, "node", [(i, (i + 1) % 32) for i in range(32)])
    codes = lax.all_to_all(codes, "node", split_axis=0, concat_axis=0, tiled=True)
    table_new, accum_new = update(place, codes, over, table, accum.reshape(32, 128))
    return table_new, accum_new.reshape(4096)


def solution(mesh):
    return jax.shard_map(
        per_device,
        mesh=mesh,
        in_specs=(
            P(("node", "local"), None),
            P(("node", "local")),
            P(("node", "local"), None),
            P(("node", "local")),
            P(("node", "local"), None),
            P(("node", "local")),
        ),
        out_specs=(P(("node", "local"), None), P(("node", "local"))),
        check_vma=False,
    )
```

```python
import jax
import jax.numpy as jnp
from jax import lax
from jax.experimental import pallas as pl
from jax.experimental.pallas import tpu as pltpu
from jax.sharding import PartitionSpec as P

LEARN_RATE = 0.3
EPSILON = 1e-06

LANES = 128
KEEP = 32
GROUP = 8
BLOCKS = 17
BUCKET_ROWS = 40
F32, BF16, I32 = jnp.float32, jnp.bfloat16, jnp.int32


def rows_iota(rows, cols):
    return lax.broadcasted_iota(I32, (rows, cols), 0)


def lanes_iota(rows, cols):
    return lax.broadcasted_iota(I32, (rows, cols), 1)


def prep_kernel(slot_ref, len_ref, pooled_ref, out_ref, perm_ref):
    slot = slot_ref[...]
    present = rows_iota(*slot.shape) < len_ref[...]
    side = (slot >> 11) & 1
    owner = (slot >> 6) & 31
    place = slot & 63
    first = place < KEEP
    low = jnp.where(first, (owner & 3) * KEEP + place, side * KEEP + place - KEEP)
    low = jnp.where(present, low, -1)
    block = (slot >> 12) * BLOCKS + jnp.where(first, side * 8 + (owner >> 2), 16)

    def by_group(x):
        parts = [x[:, LANES * b : LANES * (b + 1)] for b in range(4)]
        return jnp.concatenate(parts, axis=0).T.astype(BF16)

    out_ref[512:640, :] = by_group(low.astype(F32))
    out_ref[640:768, :] = by_group(block.astype(F32))
    for h in range(2):
        for b in range(4):
            start = b * 128 + h * 64
            perm_ref[pl.ds(h * 4 + b, 64, stride=GROUP), :] = pooled_ref[start : start + 64, :].astype(F32)
    for t in range(4):
        out_ref[t * 128 : (t + 1) * 128, :] = perm_ref[t * 128 : (t + 1) * 128, :].T.astype(BF16)


def sums_kernel(place_ref, got_ref, row_ref, own_ref, other_ref, over_ref, cross_ref, low_ref, code_ref, counts_ref):
    chip, core = place_ref[0], place_ref[1]
    for ch in range(4):
        base = ch * 768
        low_ref[ch * 128 : (ch + 1) * 128, :] = got_ref[base + 512 : base + 640, :].astype(F32)
        block = got_ref[base + 640 : base + 768, :].astype(F32).astype(I32) - chip * BLOCKS
        valid = (block >= 0) & (block < BLOCKS)
        block = jnp.where(block < 16, block ^ (core * 8), block)
        member = (rows_iota(128, 128) >> 6) * 4 + (lanes_iota(128, 128) >> 5)
        code = jnp.where(valid, block * GROUP + member, -1)
        code_ref[ch * 128 : (ch + 1) * 128, :] = code.astype(F32)

    tiles = [(rows_iota(16, 128) + 16 * t).astype(F32).astype(BF16) for t in range(9)]
    one, zero = jnp.ones((16, 128), BF16), jnp.zeros((16, 128), BF16)

    def onehot(ref, row, count):
        halves = []
        for h in range(2):
            line = ref[pl.ds(row + h * 64, 1), :]
            line = jnp.broadcast_to(line, (16, 128)).astype(BF16)
            halves.append(jnp.concatenate([jnp.where(line == tiles[t], one, zero) for t in range(count)], axis=0))
        return jnp.concatenate(halves, axis=1).astype(jnp.float8_e4m3fn)

    def group_counts(row):
        return lax.dot_general(
            onehot(code_ref, row, 9), onehot(low_ref, row, 8), (((1,), (1,)), ((), ())), preferred_element_type=F32
        )

    def step(i, carry):
        ch, pair = i // 32, i % 32
        row = ch * 128 + pair * 2
        first, second = group_counts(row), group_counts(row + 1)
        at = pl.multiple_of(i * 16, 16)
        for b in range(BLOCKS):
            both = jnp.concatenate([first[b * 8 : b * 8 + 8, :], second[b * 8 : b * 8 + 8, :]], axis=0)
            counts_ref[pl.ds(at, 16), b * 128 : (b + 1) * 128] = both.astype(BF16)
        return carry

    lax.fori_loop(0, 128, step, 0, unroll=64)

    pooled = jnp.concatenate(
        [got_ref[ch * 768 + t * 128 : ch * 768 + (t + 1) * 128, :] for ch in range(4) for t in range(4)], axis=1
    )
    total = jnp.dot(pooled, counts_ref[...], preferred_element_type=F32)
    own_ref[...] = total[:, :1024]
    other_ref[...] = total[:, 1024:2048]
    over = total[:, 2048:].T
    near = jnp.broadcast_to(core == 0, (KEEP, LANES))
    over_ref[0:32, :] = jnp.where(near, over[0:32, :], over[32:64, :])
    cross_ref[...] = jnp.where(near, over[32:64, :], over[0:32, :])
    line = row_ref[pl.ds(((place_ref[2] + 1) & 31) >> 1, 1), :] & 4095
    over_ref[32:40, :] = jnp.broadcast_to(line, (8, 128)).astype(F32)


def code_kernel(own_ref, got_ref, row_ref, out_ref):
    rows = row_ref[...] & 4095

    def coded(b):
        total = own_ref[:, b * 128 : (b + 1) * 128] + got_ref[:, b * 128 : (b + 1) * 128]
        most = jnp.max(jnp.abs(total), axis=0, keepdims=True)
        power = jnp.floor(jnp.log2(jnp.maximum(most, 1e-30))) + 1.0
        scaled = jnp.clip(jnp.round(total * jnp.exp2(15.0 - power)), -32767.0, 32767.0)
        return scaled.T.astype(I32).astype(jnp.int16), power.astype(I32)

    def tail(row_line, power_line):
        at = rows_iota(8, 128)
        out = jnp.where(at == 0, jnp.broadcast_to(row_line, (8, 128)), jnp.broadcast_to(power_line, (8, 128)))
        return out

    for b in range(8):
        codes, power = coded(b)
        for q in range(4):
            n = b * 4 + q
            out_ref[n, 0:32, :] = codes[q * 32 : (q + 1) * 32, :]
            out_ref[n, 32:40, :] = tail(rows[n >> 1 : (n >> 1) + 1, :], power).astype(jnp.int16)

def update_kernel(place_ref, got_ref, over_ref, cross_ref, table_ref, accum_ref, table_out, accum_out, value_ref, line_ref, fresh_ref, sems):
    node = place_ref[2]

    def halves(x):
        x = x.astype(I32)
        return (x >> 8).astype(F32).astype(BF16), (x & 255).astype(F32).astype(BF16)

    for m in range(32):
        high, low = halves(got_ref[m, 0:32, :])
        value_ref[m * 32 : (m + 1) * 32, 0:128] = high
        value_ref[m * 32 : (m + 1) * 32, 128:256] = low
    over = over_ref[0:32, :] + cross_ref[...]
    high = (over * (1.0 / 256.0)).astype(BF16)
    rest = over - high.astype(F32) * 256.0
    middle = rest.astype(BF16)
    value_ref[1024:1056, 0:128] = high
    value_ref[1024:1056, 128:256] = middle
    value_ref[1056:1088, 0:128] = jnp.zeros((32, 128), BF16)
    value_ref[1056:1088, 128:256] = (rest - middle.astype(F32)).astype(BF16)
    value_ref[1088:1152, :] = jnp.zeros((64, 256), BF16)

    quarter = lanes_iota(8, 128) >> 5
    ids, powers = jnp.zeros((8, 128), I32), jnp.zeros((8, 128), I32)
    for r in range(4):
        tails = [got_ref[kb * 4 + r, 32:40, :].astype(I32) for kb in range(8)]
        id_lines = jnp.concatenate([t[0:1, :] for t in tails], axis=0)
        power_lines = jnp.concatenate([t[1:2, :] for t in tails], axis=0)
        id_lines = pltpu.roll(id_lines, (r * 32 + 128 - (node & 1) * 64) & 127, axis=1)
        power_lines = pltpu.roll(power_lines, (r * 32 + 128 - (node & 3) * 32) & 127, axis=1)
        ids = jnp.where(quarter == r, id_lines, ids)
        powers = jnp.where(quarter == r, power_lines, powers)
    line_ref[0:8, :] = ids
    line_ref[8:16, :] = powers
    over_line = over_ref[32:40, :].astype(I32)
    first = pltpu.roll(over_line, (128 - ((node & 1) * 64 + 32)) & 127, axis=1)
    second = pltpu.roll(over_line, (128 - (node & 1) * 64) & 127, axis=1)
    lane = lanes_iota(8, 128)
    line_ref[16:24, :] = jnp.where(lane < 32, first, jnp.where(lane < 64, second, -1))

    tiles = [(rows_iota(16, 128) + 16 * t).astype(F32).astype(BF16) for t in range(16)]
    zero = jnp.zeros((16, 128), BF16)
    diag = rows_iota(128, 128) == lanes_iota(128, 128)
    scales = []
    for kb in range(9):
        scale = jnp.ones((1, 128), F32) if kb == 8 else jnp.exp2(line_ref[kb + 8 : kb + 9, :].astype(F32) - 15.0)
        scales.append(jnp.broadcast_to(scale, (16, 128)).astype(BF16))
    values = value_ref[...]

    copies = []
    for p in range(16):
        first_row = p * 256
        parts = []
        for kb in range(9):
            at_id = kb if kb < 8 else 16
            ids = (line_ref[at_id : at_id + 1, :] - first_row).astype(F32)
            ids = jnp.broadcast_to(ids, (16, 128)).astype(BF16)
            parts.append(jnp.concatenate([jnp.where(ids == tiles[t], scales[kb], zero) for t in range(16)], axis=0))
        hot = jnp.concatenate(parts, axis=1)
        both = jnp.dot(hot, values, preferred_element_type=F32)
        gradient = both[:, 0:128] * 256.0 + both[:, 128:256]
        for t in range(2):
            g = gradient[t * 128 : (t + 1) * 128, :]
            line = slice(p * 2 + t, p * 2 + t + 1)
            accum = jnp.broadcast_to(accum_ref[line, :], (128, 128))
            fresh = jnp.sum(g * g * (1.0 / 128.0) + jnp.where(diag, accum, 0.0), axis=1, keepdims=True)
            accum_out[line, :] = jnp.sum(jnp.where(diag, fresh, 0.0), axis=0, keepdims=True)
            step = LEARN_RATE * g / (jnp.sqrt(fresh) + EPSILON)
            at = slice(p * 256 + t * 128, p * 256 + t * 128 + 128)
            fresh_ref[at, :] = table_ref[at, :] - step
        if p % 4 == 3:
            done = pl.ds((p - 3) * 256, 1024)
            copies.append(pltpu.make_async_copy(fresh_ref.at[done, :], table_out.at[done, :], sems.at[p // 4]))
            copies[-1].start()
    for copy in copies:
        copy.wait()


VMEM = pl.BlockSpec(memory_space=pltpu.VMEM)
SMEM = pl.BlockSpec(memory_space=pltpu.SMEM)
PARAMS = pltpu.CompilerParams(vmem_limit_bytes=40 * 1024 * 1024)


def whole(*shape):
    return pl.BlockSpec(shape, lambda i: (0,) * len(shape))


def prep(slot_t, lengths, pooled):
    return pl.pallas_call(
        prep_kernel,
        grid=(1,),
        out_shape=jax.ShapeDtypeStruct((768, 128), BF16),
        in_specs=[whole(32, 512), whole(1, 512), whole(512, 128)],
        out_specs=VMEM,
        scratch_shapes=[pltpu.VMEM((512, 128), F32)],
        compiler_params=pltpu.CompilerParams(vmem_limit_bytes=63 * 1024 * 1024),
        name="prep",
    )(slot_t, lengths, pooled)


def sums(place, got, slot_row):
    return pl.pallas_call(
        sums_kernel,
        out_shape=[
            jax.ShapeDtypeStruct((128, 1024), F32),
            jax.ShapeDtypeStruct((128, 1024), F32),
            jax.ShapeDtypeStruct((40, 128), F32),
            jax.ShapeDtypeStruct((32, 128), F32),
        ],
        in_specs=[SMEM, VMEM, VMEM],
        out_specs=[VMEM] * 4,
        scratch_shapes=[
            pltpu.VMEM((512, 128), F32),
            pltpu.VMEM((512, 128), F32),
            pltpu.VMEM((2048, BLOCKS * 128), BF16),
        ],
        compiler_params=PARAMS,
        name="sums",
    )(place, got, slot_row)


def code(own, got, slot_row):
    return pl.pallas_call(
        code_kernel,
        out_shape=jax.ShapeDtypeStruct((32, BUCKET_ROWS, 128), jnp.int16),
        in_specs=[VMEM] * 3,
        out_specs=VMEM,
        compiler_params=PARAMS,
        name="code",
    )(own, got, slot_row)


def update(place, got, over, cross, table, accum):
    return pl.pallas_call(
        update_kernel,
        out_shape=[jax.ShapeDtypeStruct((4096, 128), F32), jax.ShapeDtypeStruct((32, 128), F32)],
        in_specs=[SMEM] + [VMEM] * 5,
        out_specs=[pl.BlockSpec(memory_space=pl.ANY), VMEM],
        scratch_shapes=[
            pltpu.VMEM((1152, 256), BF16),
            pltpu.VMEM((24, 128), I32),
            pltpu.VMEM((4096, 128), F32),
            pltpu.SemaphoreType.DMA((4,)),
        ],
        compiler_params=PARAMS,
        name="update",
    )(place, got, over, cross, table, accum)


def next_node(flip):
    return [(n * 8 + i, (n + 1) % 32 * 8 + (i ^ flip)) for n in range(32) for i in range(8)]


def per_device(pooled_grad, lengths, slot_of, slot_row, table, accum):
    local, node = lax.axis_index("local"), lax.axis_index("node")
    place = jnp.stack([local >> 1, local & 1, node]).astype(I32)
    packed = prep(slot_of.T, lengths.reshape(1, 512), pooled_grad)
    same_core = [[0, 2, 4, 6], [1, 3, 5, 7]]
    got = lax.all_gather(packed, "local", axis=0, tiled=True, axis_index_groups=same_core)
    rows = slot_row.reshape(16, 128)
    own, other, over, cross = sums(place, got, rows)
    other = lax.ppermute(other, "local", [(i, i ^ 1) for i in range(8)])
    over = lax.ppermute(over, ("node", "local"), next_node(0))
    cross = lax.ppermute(cross, ("node", "local"), next_node(1))
    codes = lax.all_to_all(code(own, other, rows), "node", split_axis=0, concat_axis=0, tiled=True)
    table_new, accum_new = update(place, codes, over, cross, table, accum.reshape(32, 128))
    return table_new, accum_new.reshape(4096)


def solution(mesh):
    return jax.shard_map(
        per_device,
        mesh=mesh,
        in_specs=(
            P(("node", "local"), None),
            P(("node", "local")),
            P(("node", "local"), None),
            P(("node", "local")),
            P(("node", "local"), None),
            P(("node", "local")),
        ),
        out_specs=(P(("node", "local"), None), P(("node", "local"))),
        check_vma=False,
    )
```

```python
import jax
import jax.numpy as jnp
from jax import lax
from jax.experimental import pallas as pl
from jax.experimental.pallas import tpu as pltpu
from jax.sharding import PartitionSpec as P

LEARN_RATE = 0.3
EPSILON = 1e-06

LANES = 128
KEEP = 32
GROUP = 8
BLOCKS = 17
WIDTH = BLOCKS * LANES
BUCKET_ROWS = 40
F32, BF16, I32 = jnp.float32, jnp.bfloat16, jnp.int32


def rows_iota(rows, cols):
    return lax.broadcasted_iota(I32, (rows, cols), 0)


def lanes_iota(rows, cols):
    return lax.broadcasted_iota(I32, (rows, cols), 1)


def prep_kernel(slot_ref, len_ref, pooled_ref, out_ref, perm_ref):
    slot = slot_ref[...]
    present = rows_iota(*slot.shape) < len_ref[...]
    side = (slot >> 11) & 1
    owner = (slot >> 6) & 31
    place = slot & 63
    first = place < KEEP
    low = jnp.where(first, (owner & 3) * KEEP + place, side * KEEP + place - KEEP)
    block = (slot >> 12) * BLOCKS + jnp.where(first, side * 8 + (owner >> 2), 16)

    def by_group(x):
        parts = [x[:, LANES * b : LANES * (b + 1)] for b in range(4)]
        return jnp.concatenate(parts, axis=0).T.astype(BF16)

    mark = (1.0 + low.astype(F32) * (1.0 / 128.0)) * jnp.exp2((block - 34).astype(F32))
    out_ref[512:640, :] = by_group(jnp.where(present, mark, 0.0))
    for h in range(2):
        for b in range(4):
            start = b * 128 + h * 64
            perm_ref[pl.ds(h * 4 + b, 64, stride=GROUP), :] = pooled_ref[start : start + 64, :].astype(F32)
    for t in range(4):
        out_ref[t * 128 : (t + 1) * 128, :] = perm_ref[t * 128 : (t + 1) * 128, :].T.astype(BF16)


def add_sums(place_ref, pieces, low_ref, code_ref, counts_ref):
    chip, core = place_ref[0], place_ref[1]
    span = jnp.where(chip == 0, 2.0**34, jnp.where(chip == 1, 2.0**17, jnp.where(chip == 2, 1.0, 2.0**-17))).astype(F32)
    for i, piece in enumerate(pieces):
        mark = piece(512, 640).astype(F32) * span
        valid = (mark >= 1.0) & (mark < 2.0**BLOCKS)
        power = jnp.floor(jnp.log2(jnp.maximum(mark, 0.5)) + 0.002)
        low_ref[i * 128 : (i + 1) * 128, :] = jnp.round((mark * jnp.exp2(-power) - 1.0) * 128.0)
        block = jnp.clip(power, 0.0, 16.0).astype(I32)
        block = jnp.where(block < 16, block ^ (core * 8), block)
        member = (rows_iota(128, 128) >> 6) * 4 + (lanes_iota(128, 128) >> 5)
        code_ref[i * 128 : (i + 1) * 128, :] = jnp.where(valid, block * GROUP + member, -1).astype(F32)

    tiles = [(rows_iota(16, 128) + 16 * t).astype(F32).astype(BF16) for t in range(9)]
    one, zero = jnp.ones((16, 128), BF16), jnp.zeros((16, 128), BF16)

    def onehot(ref, row, count):
        halves = []
        for h in range(2):
            line = ref[pl.ds(row + h * 64, 1), :]
            line = jnp.broadcast_to(line, (16, 128)).astype(BF16)
            halves.append(jnp.concatenate([jnp.where(line == tiles[t], one, zero) for t in range(count)], axis=0))
        return jnp.concatenate(halves, axis=1).astype(jnp.float8_e4m3fn)

    def group_counts(row):
        return lax.dot_general(
            onehot(code_ref, row, 9), onehot(low_ref, row, 8), (((1,), (1,)), ((), ())), preferred_element_type=F32
        )

    def step(i, carry):
        row = (i // 32) * 128 + (i % 32) * 2
        first, second = group_counts(row), group_counts(row + 1)
        at = pl.multiple_of(i * 16, 16)
        for b in range(BLOCKS):
            both = jnp.concatenate([first[b * 8 : b * 8 + 8, :], second[b * 8 : b * 8 + 8, :]], axis=0)
            counts_ref[pl.ds(at, 16), b * 128 : (b + 1) * 128] = both.astype(BF16)
        return carry

    lax.fori_loop(0, 32 * len(pieces), step, 0, unroll=32)
    pooled = jnp.concatenate([piece(t * 128, t * 128 + 128) for piece in pieces for t in range(4)], axis=1)
    return jnp.dot(pooled, counts_ref[...], preferred_element_type=F32)


def rows_of(ref):
    return lambda a, b: ref[a:b, :]


def own_kernel(place_ref, mine_ref, total_ref, low_ref, code_ref, counts_ref):
    total_ref[...] = add_sums(place_ref, [rows_of(mine_ref)], low_ref, code_ref, counts_ref)


def near_kernel(place_ref, left_ref, right_ref, before_ref, total_ref, low_ref, code_ref, counts_ref):
    pieces = [rows_of(left_ref), rows_of(right_ref)]
    total_ref[...] = before_ref[...] + add_sums(place_ref, pieces, low_ref, code_ref, counts_ref)


def far_kernel(place_ref, top_ref, bottom_ref, before_ref, row_ref, own_ref, other_ref, over_ref, cross_ref, low_ref, code_ref, counts_ref, far_ref):
    far_ref[0:320, :] = top_ref[...]
    far_ref[320:640, :] = bottom_ref[...]
    total = before_ref[...] + add_sums(place_ref, [rows_of(far_ref)], low_ref, code_ref, counts_ref)
    own_ref[...] = total[:, :1024]
    other_ref[...] = total[:, 1024:2048]
    over = total[:, 2048:].T
    near = jnp.broadcast_to(place_ref[1] == 0, (KEEP, LANES))
    over_ref[0:32, :] = jnp.where(near, over[0:32, :], over[32:64, :])
    cross_ref[...] = jnp.where(near, over[32:64, :], over[0:32, :])
    line = row_ref[pl.ds(((place_ref[2] + 1) & 31) >> 1, 1), :] & 4095
    over_ref[32:40, :] = jnp.broadcast_to(line, (8, 128)).astype(F32)


def code_kernel(own_ref, got_ref, row_ref, out_ref):
    rows = row_ref[...] & 4095

    def coded(b):
        total = own_ref[:, b * 128 : (b + 1) * 128] + got_ref[:, b * 128 : (b + 1) * 128]
        most = jnp.max(jnp.abs(total), axis=0, keepdims=True)
        power = jnp.floor(jnp.log2(jnp.maximum(most, 1e-30))) + 1.0
        scaled = jnp.clip(jnp.round(total * jnp.exp2(15.0 - power)), -32767.0, 32767.0)
        return scaled.T.astype(I32).astype(jnp.int16), power.astype(I32)

    def tail(row_line, power_line):
        at = rows_iota(8, 128)
        out = jnp.where(at == 0, jnp.broadcast_to(row_line, (8, 128)), jnp.broadcast_to(power_line, (8, 128)))
        return out

    for b in range(8):
        codes, power = coded(b)
        for q in range(4):
            n = b * 4 + q
            out_ref[n, 0:32, :] = codes[q * 32 : (q + 1) * 32, :]
            out_ref[n, 32:40, :] = tail(rows[n >> 1 : (n >> 1) + 1, :], power).astype(jnp.int16)

def update_kernel(place_ref, got_ref, over_ref, cross_ref, table_ref, accum_ref, table_out, accum_out, value_ref, line_ref, fresh_ref, sems):
    node = place_ref[2]

    def halves(x):
        x = x.astype(I32)
        return (x >> 8).astype(F32).astype(BF16), (x & 255).astype(F32).astype(BF16)

    for m in range(32):
        high, low = halves(got_ref[m, 0:32, :])
        value_ref[m * 32 : (m + 1) * 32, 0:128] = high
        value_ref[m * 32 : (m + 1) * 32, 128:256] = low
    over = over_ref[0:32, :] + cross_ref[...]
    high = (over * (1.0 / 256.0)).astype(BF16)
    rest = over - high.astype(F32) * 256.0
    middle = rest.astype(BF16)
    value_ref[1024:1056, 0:128] = high
    value_ref[1024:1056, 128:256] = middle
    value_ref[1056:1088, 0:128] = jnp.zeros((32, 128), BF16)
    value_ref[1056:1088, 128:256] = (rest - middle.astype(F32)).astype(BF16)
    value_ref[1088:1152, :] = jnp.zeros((64, 256), BF16)

    quarter = lanes_iota(8, 128) >> 5
    ids, powers = jnp.zeros((8, 128), I32), jnp.zeros((8, 128), I32)
    for r in range(4):
        tails = [got_ref[kb * 4 + r, 32:40, :].astype(I32) for kb in range(8)]
        id_lines = jnp.concatenate([t[0:1, :] for t in tails], axis=0)
        power_lines = jnp.concatenate([t[1:2, :] for t in tails], axis=0)
        id_lines = pltpu.roll(id_lines, (r * 32 + 128 - (node & 1) * 64) & 127, axis=1)
        power_lines = pltpu.roll(power_lines, (r * 32 + 128 - (node & 3) * 32) & 127, axis=1)
        ids = jnp.where(quarter == r, id_lines, ids)
        powers = jnp.where(quarter == r, power_lines, powers)
    line_ref[0:8, :] = ids
    line_ref[8:16, :] = powers
    over_line = over_ref[32:40, :].astype(I32)
    first = pltpu.roll(over_line, (128 - ((node & 1) * 64 + 32)) & 127, axis=1)
    second = pltpu.roll(over_line, (128 - (node & 1) * 64) & 127, axis=1)
    lane = lanes_iota(8, 128)
    line_ref[16:24, :] = jnp.where(lane < 32, first, jnp.where(lane < 64, second, -1))

    tiles = [(rows_iota(16, 128) + 16 * t).astype(F32).astype(BF16) for t in range(16)]
    zero = jnp.zeros((16, 128), BF16)
    diag = rows_iota(128, 128) == lanes_iota(128, 128)
    scales = []
    for kb in range(9):
        scale = jnp.ones((1, 128), F32) if kb == 8 else jnp.exp2(line_ref[kb + 8 : kb + 9, :].astype(F32) - 15.0)
        scales.append(jnp.broadcast_to(scale, (16, 128)).astype(BF16))
    values = value_ref[...]

    copies = []
    for p in range(16):
        first_row = p * 256
        parts = []
        for kb in range(9):
            at_id = kb if kb < 8 else 16
            ids = (line_ref[at_id : at_id + 1, :] - first_row).astype(F32)
            ids = jnp.broadcast_to(ids, (16, 128)).astype(BF16)
            parts.append(jnp.concatenate([jnp.where(ids == tiles[t], scales[kb], zero) for t in range(16)], axis=0))
        hot = jnp.concatenate(parts, axis=1)
        both = jnp.dot(hot, values, preferred_element_type=F32)
        gradient = both[:, 0:128] * 256.0 + both[:, 128:256]
        for t in range(2):
            g = gradient[t * 128 : (t + 1) * 128, :]
            line = slice(p * 2 + t, p * 2 + t + 1)
            accum = jnp.broadcast_to(accum_ref[line, :], (128, 128))
            fresh = jnp.sum(g * g * (1.0 / 128.0) + jnp.where(diag, accum, 0.0), axis=1, keepdims=True)
            accum_out[line, :] = jnp.sum(jnp.where(diag, fresh, 0.0), axis=0, keepdims=True)
            step = LEARN_RATE * g / (jnp.sqrt(fresh) + EPSILON)
            at = slice(p * 256 + t * 128, p * 256 + t * 128 + 128)
            fresh_ref[at, :] = table_ref[at, :] - step
        if p % 4 == 3:
            done = pl.ds((p - 3) * 256, 1024)
            copies.append(pltpu.make_async_copy(fresh_ref.at[done, :], table_out.at[done, :], sems.at[p // 4]))
            copies[-1].start()
    for copy in copies:
        copy.wait()


VMEM = pl.BlockSpec(memory_space=pltpu.VMEM)
SMEM = pl.BlockSpec(memory_space=pltpu.SMEM)
PARAMS = pltpu.CompilerParams(vmem_limit_bytes=40 * 1024 * 1024)


def whole(*shape):
    return pl.BlockSpec(shape, lambda i: (0,) * len(shape))


def prep(slot_t, lengths, pooled):
    return pl.pallas_call(
        prep_kernel,
        grid=(1,),
        out_shape=jax.ShapeDtypeStruct((640, 128), BF16),
        in_specs=[whole(32, 512), whole(1, 512), whole(512, 128)],
        out_specs=VMEM,
        scratch_shapes=[pltpu.VMEM((512, 128), F32)],
        compiler_params=pltpu.CompilerParams(vmem_limit_bytes=63 * 1024 * 1024),
        name="prep",
    )(slot_t, lengths, pooled)


def sums_call(kernel, name, pieces, outs, extra, *args):
    return pl.pallas_call(
        kernel,
        out_shape=[jax.ShapeDtypeStruct(shape, F32) for shape in outs],
        in_specs=[SMEM] + [VMEM] * (len(args) - 1),
        out_specs=[VMEM] * len(outs),
        scratch_shapes=[
            pltpu.VMEM((128 * pieces, 128), F32),
            pltpu.VMEM((128 * pieces, 128), F32),
            pltpu.VMEM((512 * pieces, BLOCKS * 128), BF16),
        ]
        + extra,
        compiler_params=PARAMS,
        cost_estimate=pl.CostEstimate(flops=2_000_000_000 * pieces, bytes_accessed=3_000_000, transcendentals=0),
        name=name,
    )(*args)


def gather_sums(place, packed, rows):
    shift = lambda x, k: lax.ppermute(x, "local", [(i, (i + k) % 8) for i in range(8)])
    left, right = shift(packed, 2), shift(packed, 6)
    (total,) = sums_call(own_kernel, "own_sums", 1, [(128, WIDTH)], [], place, packed)
    left, right, total = lax.optimization_barrier((left, right, total))
    top, bottom = shift(left[:320], 2), shift(right[320:], 6)
    (total,) = sums_call(near_kernel, "near_sums", 2, [(128, WIDTH)], [], place, left, right, total)
    outs = [(128, 1024), (128, 1024), (40, 128), (32, 128)]
    return sums_call(far_kernel, "far_sums", 1, outs, [pltpu.VMEM((640, 128), BF16)], place, top, bottom, total, rows)


def code(own, got, slot_row):
    return pl.pallas_call(
        code_kernel,
        out_shape=jax.ShapeDtypeStruct((32, BUCKET_ROWS, 128), jnp.int16),
        in_specs=[VMEM] * 3,
        out_specs=VMEM,
        compiler_params=PARAMS,
        name="code",
    )(own, got, slot_row)


def update(place, got, over, cross, table, accum):
    return pl.pallas_call(
        update_kernel,
        out_shape=[jax.ShapeDtypeStruct((4096, 128), F32), jax.ShapeDtypeStruct((32, 128), F32)],
        in_specs=[SMEM] + [VMEM] * 5,
        out_specs=[pl.BlockSpec(memory_space=pl.ANY), VMEM],
        scratch_shapes=[
            pltpu.VMEM((1152, 256), BF16),
            pltpu.VMEM((24, 128), I32),
            pltpu.VMEM((4096, 128), F32),
            pltpu.SemaphoreType.DMA((4,)),
        ],
        compiler_params=PARAMS,
        name="update",
    )(place, got, over, cross, table, accum)


def next_node(flip):
    return [(n * 8 + i, (n + 1) % 32 * 8 + (i ^ flip)) for n in range(32) for i in range(8)]


def per_device(pooled_grad, lengths, slot_of, slot_row, table, accum):
    local, node = lax.axis_index("local"), lax.axis_index("node")
    place = jnp.stack([local >> 1, local & 1, node]).astype(I32)
    packed = prep(slot_of.T, lengths.reshape(1, 512), pooled_grad)
    rows = slot_row.reshape(16, 128)
    own, other, over, cross = gather_sums(place, packed, rows)
    other = lax.ppermute(other, "local", [(i, i ^ 1) for i in range(8)])
    over = lax.ppermute(over, ("node", "local"), next_node(0))
    cross = lax.ppermute(cross, ("node", "local"), next_node(1))
    codes, over, cross = lax.optimization_barrier((code(own, other, rows), over, cross))
    codes = lax.all_to_all(codes, "node", split_axis=0, concat_axis=0, tiled=True)
    table_new, accum_new = update(place, codes, over, cross, table, accum.reshape(32, 128))
    return table_new, accum_new.reshape(4096)


def solution(mesh):
    return jax.shard_map(
        per_device,
        mesh=mesh,
        in_specs=(
            P(("node", "local"), None),
            P(("node", "local")),
            P(("node", "local"), None),
            P(("node", "local")),
            P(("node", "local"), None),
            P(("node", "local")),
        ),
        out_specs=(P(("node", "local"), None), P(("node", "local"))),
        check_vma=False,
    )
```

```python
import jax
import jax.numpy as jnp
from jax import lax
from jax.experimental import pallas as pl
from jax.experimental.pallas import tpu as pltpu
from jax.sharding import PartitionSpec as P

LEARN_RATE = 0.3
EPSILON = 1e-06

LANES = 128
KEEP = 32
GROUP = 8
BLOCKS = 17
WIDTH = BLOCKS * LANES
BUCKET_ROWS = 40
F32, BF16, I32 = jnp.float32, jnp.bfloat16, jnp.int32


def rows_iota(rows, cols):
    return lax.broadcasted_iota(I32, (rows, cols), 0)


def lanes_iota(rows, cols):
    return lax.broadcasted_iota(I32, (rows, cols), 1)


def prep_kernel(slot_ref, len_ref, pooled_ref, out_ref, perm_ref):
    slot = slot_ref[...]
    present = rows_iota(*slot.shape) < len_ref[...]
    side = (slot >> 11) & 1
    owner = (slot >> 6) & 31
    place = slot & 63
    first = place < KEEP
    low = jnp.where(first, (owner & 3) * KEEP + place, side * KEEP + place - KEEP)
    block = (slot >> 12) * BLOCKS + jnp.where(first, side * 8 + (owner >> 2), 16)

    def by_group(x):
        parts = [x[:, LANES * b : LANES * (b + 1)] for b in range(4)]
        return jnp.concatenate(parts, axis=0).T.astype(BF16)

    mark = (1.0 + low.astype(F32) * (1.0 / 128.0)) * jnp.exp2((block - 34).astype(F32))
    out_ref[512:640, :] = by_group(jnp.where(present, mark, 0.0))
    for h in range(2):
        for b in range(4):
            start = b * 128 + h * 64
            perm_ref[pl.ds(h * 4 + b, 64, stride=GROUP), :] = pooled_ref[start : start + 64, :].astype(F32)
    for t in range(4):
        out_ref[t * 128 : (t + 1) * 128, :] = perm_ref[t * 128 : (t + 1) * 128, :].T.astype(BF16)


def add_sums(place_ref, piece, low_ref, code_ref, counts_ref):
    chip, core = place_ref[0], place_ref[1]
    span = jnp.where(chip == 0, 2.0**34, jnp.where(chip == 1, 2.0**17, jnp.where(chip == 2, 1.0, 2.0**-17))).astype(F32)
    mark = piece(512, 640).astype(F32) * span
    valid = (mark >= 1.0) & (mark < 2.0**BLOCKS)
    power = jnp.floor(jnp.log2(jnp.maximum(mark, 0.5)) + 0.002)
    low_ref[...] = jnp.round((mark * jnp.exp2(-power) - 1.0) * 128.0)
    block = jnp.clip(power, 0.0, 16.0).astype(I32)
    block = jnp.where(block < 16, block ^ (core * 8), block)
    member = (rows_iota(128, 128) >> 6) * 4 + (lanes_iota(128, 128) >> 5)
    code_ref[...] = jnp.where(valid, block * GROUP + member, -1).astype(F32)

    tiles = [(rows_iota(16, 128) + 16 * t).astype(F32).astype(BF16) for t in range(9)]
    one, zero = jnp.ones((16, 128), BF16), jnp.zeros((16, 128), BF16)

    def onehot(ref, row, count):
        halves = []
        for h in range(2):
            line = ref[pl.ds(row + h * 64, 1), :]
            line = jnp.broadcast_to(line, (16, 128)).astype(BF16)
            halves.append(jnp.concatenate([jnp.where(line == tiles[t], one, zero) for t in range(count)], axis=0))
        return jnp.concatenate(halves, axis=1).astype(jnp.float8_e4m3fn)

    def group_counts(row):
        return lax.dot_general(
            onehot(code_ref, row, 9), onehot(low_ref, row, 8), (((1,), (1,)), ((), ())), preferred_element_type=F32
        )

    def step(i, carry):
        first, second = group_counts(i * 2), group_counts(i * 2 + 1)
        at = pl.multiple_of(i * 16, 16)
        for b in range(BLOCKS):
            both = jnp.concatenate([first[b * 8 : b * 8 + 8, :], second[b * 8 : b * 8 + 8, :]], axis=0)
            counts_ref[pl.ds(at, 16), b * 128 : (b + 1) * 128] = both.astype(BF16)
        return carry

    lax.fori_loop(0, 32, step, 0, unroll=32)
    pooled = jnp.concatenate([piece(t * 128, t * 128 + 128) for t in range(4)], axis=1)
    return jnp.dot(pooled, counts_ref[...], preferred_element_type=F32)


def rows_of(ref):
    return lambda a, b: ref[a:b, :]


def own_kernel(place_ref, mine_ref, total_ref, low_ref, code_ref, counts_ref):
    total_ref[...] = add_sums(place_ref, rows_of(mine_ref), low_ref, code_ref, counts_ref)


def near_kernel(place_ref, near_ref, before_ref, total_ref, low_ref, code_ref, counts_ref):
    total_ref[...] = before_ref[...] + add_sums(place_ref, rows_of(near_ref), low_ref, code_ref, counts_ref)


def far_kernel(place_ref, far_ref, before_ref, row_ref, own_ref, other_ref, over_ref, cross_ref, low_ref, code_ref, counts_ref):
    total = before_ref[...] + add_sums(place_ref, rows_of(far_ref), low_ref, code_ref, counts_ref)
    own_ref[...] = total[:, :1024]
    other_ref[...] = total[:, 1024:2048]
    over = total[:, 2048:].T
    near = jnp.broadcast_to(place_ref[1] == 0, (KEEP, LANES))
    over_ref[0:32, :] = jnp.where(near, over[0:32, :], over[32:64, :])
    cross_ref[...] = jnp.where(near, over[32:64, :], over[0:32, :])
    line = row_ref[pl.ds(((place_ref[2] + 1) & 31) >> 1, 1), :] & 4095
    over_ref[32:40, :] = jnp.broadcast_to(line, (8, 128)).astype(F32)


def code_kernel(own_ref, got_ref, row_ref, out_ref):
    rows = row_ref[...] & 4095

    def coded(b):
        total = own_ref[:, b * 128 : (b + 1) * 128] + got_ref[:, b * 128 : (b + 1) * 128]
        most = jnp.max(jnp.abs(total), axis=0, keepdims=True)
        power = jnp.floor(jnp.log2(jnp.maximum(most, 1e-30))) + 1.0
        scaled = jnp.clip(jnp.round(total * jnp.exp2(15.0 - power)), -32767.0, 32767.0)
        return scaled.T.astype(I32).astype(jnp.int16), power.astype(I32)

    def tail(row_line, power_line):
        at = rows_iota(8, 128)
        out = jnp.where(at == 0, jnp.broadcast_to(row_line, (8, 128)), jnp.broadcast_to(power_line, (8, 128)))
        return out

    for b in range(8):
        codes, power = coded(b)
        for q in range(4):
            n = b * 4 + q
            out_ref[n, 0:32, :] = codes[q * 32 : (q + 1) * 32, :]
            out_ref[n, 32:40, :] = tail(rows[n >> 1 : (n >> 1) + 1, :], power).astype(jnp.int16)

def update_kernel(place_ref, got_ref, over_ref, cross_ref, table_ref, accum_ref, table_out, accum_out, value_ref, line_ref, fresh_ref, sems):
    node = place_ref[2]

    def halves(x):
        x = x.astype(I32)
        return (x >> 8).astype(F32).astype(BF16), (x & 255).astype(F32).astype(BF16)

    for m in range(32):
        high, low = halves(got_ref[m, 0:32, :])
        value_ref[m * 32 : (m + 1) * 32, 0:128] = high
        value_ref[m * 32 : (m + 1) * 32, 128:256] = low
    over = over_ref[0:32, :] + cross_ref[...]
    high = (over * (1.0 / 256.0)).astype(BF16)
    rest = over - high.astype(F32) * 256.0
    middle = rest.astype(BF16)
    value_ref[1024:1056, 0:128] = high
    value_ref[1024:1056, 128:256] = middle
    value_ref[1056:1088, 0:128] = jnp.zeros((32, 128), BF16)
    value_ref[1056:1088, 128:256] = (rest - middle.astype(F32)).astype(BF16)
    value_ref[1088:1152, :] = jnp.zeros((64, 256), BF16)

    quarter = lanes_iota(8, 128) >> 5
    ids, powers = jnp.zeros((8, 128), I32), jnp.zeros((8, 128), I32)
    for r in range(4):
        tails = [got_ref[kb * 4 + r, 32:40, :].astype(I32) for kb in range(8)]
        id_lines = jnp.concatenate([t[0:1, :] for t in tails], axis=0)
        power_lines = jnp.concatenate([t[1:2, :] for t in tails], axis=0)
        id_lines = pltpu.roll(id_lines, (r * 32 + 128 - (node & 1) * 64) & 127, axis=1)
        power_lines = pltpu.roll(power_lines, (r * 32 + 128 - (node & 3) * 32) & 127, axis=1)
        ids = jnp.where(quarter == r, id_lines, ids)
        powers = jnp.where(quarter == r, power_lines, powers)
    line_ref[0:8, :] = ids
    line_ref[8:16, :] = powers
    over_line = over_ref[32:40, :].astype(I32)
    first = pltpu.roll(over_line, (128 - ((node & 1) * 64 + 32)) & 127, axis=1)
    second = pltpu.roll(over_line, (128 - (node & 1) * 64) & 127, axis=1)
    lane = lanes_iota(8, 128)
    line_ref[16:24, :] = jnp.where(lane < 32, first, jnp.where(lane < 64, second, -1))

    tiles = [(rows_iota(16, 128) + 16 * t).astype(F32).astype(BF16) for t in range(16)]
    zero = jnp.zeros((16, 128), BF16)
    diag = rows_iota(128, 128) == lanes_iota(128, 128)
    scales = []
    for kb in range(9):
        scale = jnp.ones((1, 128), F32) if kb == 8 else jnp.exp2(line_ref[kb + 8 : kb + 9, :].astype(F32) - 15.0)
        scales.append(jnp.broadcast_to(scale, (16, 128)).astype(BF16))
    values = value_ref[...]

    copies = []
    for p in range(16):
        first_row = p * 256
        parts = []
        for kb in range(9):
            at_id = kb if kb < 8 else 16
            ids = (line_ref[at_id : at_id + 1, :] - first_row).astype(F32)
            ids = jnp.broadcast_to(ids, (16, 128)).astype(BF16)
            parts.append(jnp.concatenate([jnp.where(ids == tiles[t], scales[kb], zero) for t in range(16)], axis=0))
        hot = jnp.concatenate(parts, axis=1)
        both = jnp.dot(hot, values, preferred_element_type=F32)
        gradient = both[:, 0:128] * 256.0 + both[:, 128:256]
        for t in range(2):
            g = gradient[t * 128 : (t + 1) * 128, :]
            line = slice(p * 2 + t, p * 2 + t + 1)
            accum = jnp.broadcast_to(accum_ref[line, :], (128, 128))
            fresh = jnp.sum(g * g * (1.0 / 128.0) + jnp.where(diag, accum, 0.0), axis=1, keepdims=True)
            accum_out[line, :] = jnp.sum(jnp.where(diag, fresh, 0.0), axis=0, keepdims=True)
            step = g * (LEARN_RATE / (jnp.sqrt(fresh) + EPSILON))
            at = slice(p * 256 + t * 128, p * 256 + t * 128 + 128)
            fresh_ref[at, :] = table_ref[at, :] - step
        if p in (9, 13, 15):
            first = {9: 0, 13: 10, 15: 14}[p]
            done = pl.ds(first * 256, (p + 1 - first) * 256)
            copies.append(pltpu.make_async_copy(fresh_ref.at[done, :], table_out.at[done, :], sems.at[len(copies)]))
            copies[-1].start()
    for copy in copies:
        copy.wait()


VMEM = pl.BlockSpec(memory_space=pltpu.VMEM)
SMEM = pl.BlockSpec(memory_space=pltpu.SMEM)
PARAMS = pltpu.CompilerParams(vmem_limit_bytes=40 * 1024 * 1024)


def whole(*shape):
    return pl.BlockSpec(shape, lambda i: (0,) * len(shape))


def prep(slot_t, lengths, pooled):
    return pl.pallas_call(
        prep_kernel,
        grid=(1,),
        out_shape=jax.ShapeDtypeStruct((640, 128), BF16),
        in_specs=[whole(32, 512), whole(1, 512), whole(512, 128)],
        out_specs=VMEM,
        scratch_shapes=[pltpu.VMEM((512, 128), F32)],
        compiler_params=pltpu.CompilerParams(vmem_limit_bytes=63 * 1024 * 1024),
        name="prep",
    )(slot_t, lengths, pooled)


def sums_call(kernel, name, outs, *args):
    return pl.pallas_call(
        kernel,
        out_shape=[jax.ShapeDtypeStruct(shape, F32) for shape in outs],
        in_specs=[SMEM] + [VMEM] * (len(args) - 1),
        out_specs=[VMEM] * len(outs),
        scratch_shapes=[pltpu.VMEM((128, 128), F32), pltpu.VMEM((128, 128), F32), pltpu.VMEM((512, WIDTH), BF16)],
        compiler_params=PARAMS,
        cost_estimate=pl.CostEstimate(flops=2_000_000_000, bytes_accessed=3_000_000, transcendentals=0),
        name=name,
    )(*args)


def gather_sums(place, packed, rows):
    shift = lambda x, k: lax.ppermute(x, "local", [(i, (i + k) % 8) for i in range(8)])
    right = shift(packed, 6)
    (total,) = sums_call(own_kernel, "own_sums", [(128, WIDTH)], place, packed)
    packed, total = lax.optimization_barrier((packed, total))
    left = shift(packed, 2)
    right, total = lax.optimization_barrier((right, total))
    far = shift(right, 6)
    (total,) = sums_call(near_kernel, "right_sums", [(128, WIDTH)], place, right, total)
    left, total = lax.optimization_barrier((left, total))
    (total,) = sums_call(near_kernel, "left_sums", [(128, WIDTH)], place, left, total)
    outs = [(128, 1024), (128, 1024), (40, 128), (32, 128)]
    return sums_call(far_kernel, "far_sums", outs, place, far, total, rows)


def code(own, got, slot_row):
    return pl.pallas_call(
        code_kernel,
        out_shape=jax.ShapeDtypeStruct((32, BUCKET_ROWS, 128), jnp.int16),
        in_specs=[VMEM] * 3,
        out_specs=VMEM,
        compiler_params=PARAMS,
        name="code",
    )(own, got, slot_row)


def update(place, got, over, cross, table, accum):
    return pl.pallas_call(
        update_kernel,
        out_shape=[jax.ShapeDtypeStruct((4096, 128), F32), jax.ShapeDtypeStruct((32, 128), F32)],
        in_specs=[SMEM] + [VMEM] * 5,
        out_specs=[pl.BlockSpec(memory_space=pl.ANY), VMEM],
        scratch_shapes=[
            pltpu.VMEM((1152, 256), BF16),
            pltpu.VMEM((24, 128), I32),
            pltpu.VMEM((4096, 128), F32),
            pltpu.SemaphoreType.DMA((3,)),
        ],
        compiler_params=PARAMS,
        name="update",
    )(place, got, over, cross, table, accum)


def next_node(flip):
    return [(n * 8 + i, (n + 1) % 32 * 8 + (i ^ flip)) for n in range(32) for i in range(8)]


def per_device(pooled_grad, lengths, slot_of, slot_row, table, accum):
    local, node = lax.axis_index("local"), lax.axis_index("node")
    place = jnp.stack([local >> 1, local & 1, node]).astype(I32)
    packed = prep(slot_of.T, lengths.reshape(1, 512), pooled_grad)
    rows = slot_row.reshape(16, 128)
    own, other, over, cross = gather_sums(place, packed, rows)
    other = lax.ppermute(other, "local", [(i, i ^ 1) for i in range(8)])
    over = lax.ppermute(over, ("node", "local"), next_node(0))
    cross = lax.ppermute(cross, ("node", "local"), next_node(1))
    codes = lax.all_to_all(code(own, other, rows), "node", split_axis=0, concat_axis=0, tiled=True)
    table_new, accum_new = update(place, codes, over, cross, table, accum.reshape(32, 128))
    return table_new, accum_new.reshape(4096)


def solution(mesh):
    return jax.shard_map(
        per_device,
        mesh=mesh,
        in_specs=(
            P(("node", "local"), None),
            P(("node", "local")),
            P(("node", "local"), None),
            P(("node", "local")),
            P(("node", "local"), None),
            P(("node", "local")),
        ),
        out_specs=(P(("node", "local"), None), P(("node", "local"))),
        check_vma=False,
    )
```

```python
import jax
import jax.numpy as jnp
from jax import lax
from jax.experimental import pallas as pl
from jax.experimental.pallas import tpu as pltpu
from jax.sharding import PartitionSpec as P

LEARN_RATE = 0.3
EPSILON = 1e-06

LANES = 128
KEEP = 32
GROUP = 8
BLOCKS = 17
WIDTH = BLOCKS * LANES
BUCKET_ROWS = 40
F32, BF16, I32 = jnp.float32, jnp.bfloat16, jnp.int32


def rows_iota(rows, cols):
    return lax.broadcasted_iota(I32, (rows, cols), 0)


def lanes_iota(rows, cols):
    return lax.broadcasted_iota(I32, (rows, cols), 1)


def prep_kernel(slot_ref, len_ref, pooled_ref, out_ref, perm_ref):
    slot = slot_ref[...]
    present = rows_iota(*slot.shape) < len_ref[...]
    side = (slot >> 11) & 1
    owner = (slot >> 6) & 31
    place = slot & 63
    first = place < KEEP
    low = jnp.where(first, (owner & 3) * KEEP + place, side * KEEP + place - KEEP)
    block = (slot >> 12) * BLOCKS + jnp.where(first, side * 8 + (owner >> 2), 16)

    def by_group(x):
        parts = [x[:, LANES * b : LANES * (b + 1)] for b in range(4)]
        return jnp.concatenate(parts, axis=0).T.astype(BF16)

    mark = (1.0 + low.astype(F32) * (1.0 / 128.0)) * jnp.exp2((block - 34).astype(F32))
    out_ref[512:640, :] = by_group(jnp.where(present, mark, 0.0))
    for h in range(2):
        for b in range(4):
            start = b * 128 + h * 64
            perm_ref[pl.ds(h * 4 + b, 64, stride=GROUP), :] = pooled_ref[start : start + 64, :].astype(F32)
    for t in range(4):
        out_ref[t * 128 : (t + 1) * 128, :] = perm_ref[t * 128 : (t + 1) * 128, :].T.astype(BF16)


def add_sums(place_ref, pieces, low_ref, code_ref, counts_ref):
    chip, core = place_ref[0], place_ref[1]
    span = jnp.where(chip == 0, 2.0**34, jnp.where(chip == 1, 2.0**17, jnp.where(chip == 2, 1.0, 2.0**-17))).astype(F32)
    mark = jnp.concatenate([piece(512, 640) for piece in pieces], axis=0).astype(F32) * span
    valid = (mark >= 1.0) & (mark < 2.0**BLOCKS)
    power = jnp.floor(jnp.log2(jnp.maximum(mark, 0.5)) + 0.002)
    low_ref[...] = jnp.round((mark * jnp.exp2(-power) - 1.0) * 128.0)
    block = jnp.clip(power, 0.0, 16.0).astype(I32)
    block = jnp.where(block < 16, block ^ (core * 8), block)
    member = ((rows_iota(*mark.shape) >> 6) & 1) * 4 + (lanes_iota(*mark.shape) >> 5)
    code_ref[...] = jnp.where(valid, block * GROUP + member, -1).astype(F32)

    tiles = [(rows_iota(16, 128) + 16 * t).astype(F32).astype(BF16) for t in range(9)]
    one, zero = jnp.ones((16, 128), BF16), jnp.zeros((16, 128), BF16)

    def onehot(ref, row, count):
        halves = []
        for h in range(2):
            line = ref[pl.ds(row + h * 64, 1), :]
            line = jnp.broadcast_to(line, (16, 128)).astype(BF16)
            halves.append(jnp.concatenate([jnp.where(line == tiles[t], one, zero) for t in range(count)], axis=0))
        return jnp.concatenate(halves, axis=1).astype(jnp.float8_e4m3fn)

    def group_counts(row):
        return lax.dot_general(
            onehot(code_ref, row, 9), onehot(low_ref, row, 8), (((1,), (1,)), ((), ())), preferred_element_type=F32
        )

    def step(i, carry):
        row = (i // 32) * 128 + (i % 32) * 2
        first, second = group_counts(row), group_counts(row + 1)
        at = pl.multiple_of(i * 16, 16)
        for b in range(BLOCKS):
            both = jnp.concatenate([first[b * 8 : b * 8 + 8, :], second[b * 8 : b * 8 + 8, :]], axis=0)
            counts_ref[pl.ds(at, 16), b * 128 : (b + 1) * 128] = both.astype(BF16)
        return carry

    lax.fori_loop(0, 32 * len(pieces), step, 0, unroll=32)
    pooled = jnp.concatenate([piece(t * 128, t * 128 + 128) for piece in pieces for t in range(4)], axis=1)
    return jnp.dot(pooled, counts_ref[...], preferred_element_type=F32)


def rows_of(ref):
    return lambda a, b: ref[a:b, :]


def own_kernel(place_ref, mine_ref, total_ref, low_ref, code_ref, counts_ref):
    total_ref[...] = add_sums(place_ref, [rows_of(mine_ref)], low_ref, code_ref, counts_ref)


def near_kernel(place_ref, near_ref, before_ref, total_ref, low_ref, code_ref, counts_ref):
    total_ref[...] = before_ref[...] + add_sums(place_ref, [rows_of(near_ref)], low_ref, code_ref, counts_ref)


def far_kernel(place_ref, right_ref, far_ref, before_ref, row_ref, own_ref, other_ref, over_ref, cross_ref, low_ref, code_ref, counts_ref):
    total = before_ref[...] + add_sums(place_ref, [rows_of(right_ref), rows_of(far_ref)], low_ref, code_ref, counts_ref)
    own_ref[...] = total[:, :1024]
    other_ref[...] = total[:, 1024:2048]
    over = total[:, 2048:].T
    near = jnp.broadcast_to(place_ref[1] == 0, (KEEP, LANES))
    over_ref[0:32, :] = jnp.where(near, over[0:32, :], over[32:64, :])
    cross_ref[...] = jnp.where(near, over[32:64, :], over[0:32, :])
    line = row_ref[pl.ds(((place_ref[2] + 1) & 31) >> 1, 1), :] & 4095
    over_ref[32:40, :] = jnp.broadcast_to(line, (8, 128)).astype(F32)


def code_kernel(own_ref, got_ref, row_ref, out_ref):
    rows = row_ref[...] & 4095

    def coded(b):
        total = own_ref[:, b * 128 : (b + 1) * 128] + got_ref[:, b * 128 : (b + 1) * 128]
        most = jnp.max(jnp.abs(total), axis=0, keepdims=True)
        power = jnp.floor(jnp.log2(jnp.maximum(most, 1e-30))) + 1.0
        scaled = jnp.clip(jnp.round(total * jnp.exp2(15.0 - power)), -32767.0, 32767.0)
        return scaled.T.astype(I32).astype(jnp.int16), power.astype(I32)

    def tail(row_line, power_line):
        at = rows_iota(8, 128)
        out = jnp.where(at == 0, jnp.broadcast_to(row_line, (8, 128)), jnp.broadcast_to(power_line, (8, 128)))
        return out

    for b in range(8):
        codes, power = coded(b)
        for q in range(4):
            n = b * 4 + q
            out_ref[n, 0:32, :] = codes[q * 32 : (q + 1) * 32, :]
            out_ref[n, 32:40, :] = tail(rows[n >> 1 : (n >> 1) + 1, :], power).astype(jnp.int16)

def update_kernel(place_ref, got_ref, over_ref, cross_ref, table_ref, accum_ref, table_out, accum_out, value_ref, line_ref, fresh_ref, sems):
    node = place_ref[2]

    def halves(x):
        x = x.astype(I32)
        return (x >> 8).astype(F32).astype(BF16), (x & 255).astype(F32).astype(BF16)

    for m in range(32):
        high, low = halves(got_ref[m, 0:32, :])
        value_ref[m * 32 : (m + 1) * 32, 0:128] = high
        value_ref[m * 32 : (m + 1) * 32, 128:256] = low
    over = over_ref[0:32, :] + cross_ref[...]
    high = (over * (1.0 / 256.0)).astype(BF16)
    rest = over - high.astype(F32) * 256.0
    middle = rest.astype(BF16)
    value_ref[1024:1056, 0:128] = high
    value_ref[1024:1056, 128:256] = middle
    value_ref[1056:1088, 0:128] = jnp.zeros((32, 128), BF16)
    value_ref[1056:1088, 128:256] = (rest - middle.astype(F32)).astype(BF16)
    value_ref[1088:1152, :] = jnp.zeros((64, 256), BF16)

    quarter = lanes_iota(8, 128) >> 5
    ids, powers = jnp.zeros((8, 128), I32), jnp.zeros((8, 128), I32)
    for r in range(4):
        tails = [got_ref[kb * 4 + r, 32:40, :].astype(I32) for kb in range(8)]
        id_lines = jnp.concatenate([t[0:1, :] for t in tails], axis=0)
        power_lines = jnp.concatenate([t[1:2, :] for t in tails], axis=0)
        id_lines = pltpu.roll(id_lines, (r * 32 + 128 - (node & 1) * 64) & 127, axis=1)
        power_lines = pltpu.roll(power_lines, (r * 32 + 128 - (node & 3) * 32) & 127, axis=1)
        ids = jnp.where(quarter == r, id_lines, ids)
        powers = jnp.where(quarter == r, power_lines, powers)
    line_ref[0:8, :] = ids
    line_ref[8:16, :] = powers
    over_line = over_ref[32:40, :].astype(I32)
    first = pltpu.roll(over_line, (128 - ((node & 1) * 64 + 32)) & 127, axis=1)
    second = pltpu.roll(over_line, (128 - (node & 1) * 64) & 127, axis=1)
    lane = lanes_iota(8, 128)
    line_ref[16:24, :] = jnp.where(lane < 32, first, jnp.where(lane < 64, second, -1))

    tiles = [(rows_iota(16, 128) + 16 * t).astype(F32).astype(BF16) for t in range(16)]
    zero = jnp.zeros((16, 128), BF16)
    diag = rows_iota(128, 128) == lanes_iota(128, 128)
    scales = []
    for kb in range(9):
        scale = jnp.ones((1, 128), F32) if kb == 8 else jnp.exp2(line_ref[kb + 8 : kb + 9, :].astype(F32) - 15.0)
        scales.append(jnp.broadcast_to(scale, (16, 128)).astype(BF16))
    values = value_ref[...]

    copies = []
    for p in range(16):
        first_row = p * 256
        parts = []
        for kb in range(9):
            at_id = kb if kb < 8 else 16
            ids = (line_ref[at_id : at_id + 1, :] - first_row).astype(F32)
            ids = jnp.broadcast_to(ids, (16, 128)).astype(BF16)
            parts.append(jnp.concatenate([jnp.where(ids == tiles[t], scales[kb], zero) for t in range(16)], axis=0))
        hot = jnp.concatenate(parts, axis=1)
        both = jnp.dot(hot, values, preferred_element_type=F32)
        gradient = both[:, 0:128] * 256.0 + both[:, 128:256]
        for t in range(2):
            g = gradient[t * 128 : (t + 1) * 128, :]
            line = slice(p * 2 + t, p * 2 + t + 1)
            accum = jnp.broadcast_to(accum_ref[line, :], (128, 128))
            fresh = jnp.sum(g * g * (1.0 / 128.0) + jnp.where(diag, accum, 0.0), axis=1, keepdims=True)
            accum_out[line, :] = jnp.sum(jnp.where(diag, fresh, 0.0), axis=0, keepdims=True)
            step = g * (LEARN_RATE / (jnp.sqrt(fresh) + EPSILON))
            at = slice(p * 256 + t * 128, p * 256 + t * 128 + 128)
            fresh_ref[at, :] = table_ref[at, :] - step
        if p in (9, 13, 15):
            first = {9: 0, 13: 10, 15: 14}[p]
            done = pl.ds(first * 256, (p + 1 - first) * 256)
            copies.append(pltpu.make_async_copy(fresh_ref.at[done, :], table_out.at[done, :], sems.at[len(copies)]))
            copies[-1].start()
    for copy in copies:
        copy.wait()


VMEM = pl.BlockSpec(memory_space=pltpu.VMEM)
SMEM = pl.BlockSpec(memory_space=pltpu.SMEM)
PARAMS = pltpu.CompilerParams(vmem_limit_bytes=40 * 1024 * 1024)


def whole(*shape):
    return pl.BlockSpec(shape, lambda i: (0,) * len(shape))


def prep(slot_t, lengths, pooled):
    return pl.pallas_call(
        prep_kernel,
        grid=(1,),
        out_shape=jax.ShapeDtypeStruct((640, 128), BF16),
        in_specs=[whole(32, 512), whole(1, 512), whole(512, 128)],
        out_specs=VMEM,
        scratch_shapes=[pltpu.VMEM((512, 128), F32)],
        compiler_params=pltpu.CompilerParams(vmem_limit_bytes=63 * 1024 * 1024),
        name="prep",
    )(slot_t, lengths, pooled)


def sums_call(kernel, name, pieces, outs, *args):
    return pl.pallas_call(
        kernel,
        out_shape=[jax.ShapeDtypeStruct(shape, F32) for shape in outs],
        in_specs=[SMEM] + [VMEM] * (len(args) - 1),
        out_specs=[VMEM] * len(outs),
        scratch_shapes=[pltpu.VMEM((128 * pieces, 128), F32), pltpu.VMEM((128 * pieces, 128), F32), pltpu.VMEM((512 * pieces, WIDTH), BF16)],
        compiler_params=PARAMS,
        cost_estimate=pl.CostEstimate(flops=2_000_000_000 * pieces, bytes_accessed=3_000_000, transcendentals=0),
        name=name,
    )(*args)


def gather_sums(place, packed, rows):
    shift = lambda x, k: lax.ppermute(x, "local", [(i, (i + k) % 8) for i in range(8)])
    left, right, far = shift(packed, 2), shift(packed, 6), shift(packed, 4)
    (total,) = sums_call(own_kernel, "own_sums", 1, [(128, WIDTH)], place, packed)
    left, total = lax.optimization_barrier((left, total))
    (total,) = sums_call(near_kernel, "left_sums", 1, [(128, WIDTH)], place, left, total)
    outs = [(128, 1024), (128, 1024), (40, 128), (32, 128)]
    return sums_call(far_kernel, "far_sums", 2, outs, place, right, far, total, rows)


def code(own, got, slot_row):
    return pl.pallas_call(
        code_kernel,
        out_shape=jax.ShapeDtypeStruct((32, BUCKET_ROWS, 128), jnp.int16),
        in_specs=[VMEM] * 3,
        out_specs=VMEM,
        compiler_params=PARAMS,
        name="code",
    )(own, got, slot_row)


def update(place, got, over, cross, table, accum):
    return pl.pallas_call(
        update_kernel,
        out_shape=[jax.ShapeDtypeStruct((4096, 128), F32), jax.ShapeDtypeStruct((32, 128), F32)],
        in_specs=[SMEM] + [VMEM] * 5,
        out_specs=[pl.BlockSpec(memory_space=pl.ANY), VMEM],
        scratch_shapes=[
            pltpu.VMEM((1152, 256), BF16),
            pltpu.VMEM((24, 128), I32),
            pltpu.VMEM((4096, 128), F32),
            pltpu.SemaphoreType.DMA((3,)),
        ],
        compiler_params=PARAMS,
        name="update",
    )(place, got, over, cross, table, accum)


def next_node(flip):
    return [(n * 8 + i, (n + 1) % 32 * 8 + (i ^ flip)) for n in range(32) for i in range(8)]


def per_device(pooled_grad, lengths, slot_of, slot_row, table, accum):
    local, node = lax.axis_index("local"), lax.axis_index("node")
    place = jnp.stack([local >> 1, local & 1, node]).astype(I32)
    packed = prep(slot_of.T, lengths.reshape(1, 512), pooled_grad)
    rows = slot_row.reshape(16, 128)
    own, other, over, cross = gather_sums(place, packed, rows)
    other = lax.ppermute(other, "local", [(i, i ^ 1) for i in range(8)])
    over = lax.ppermute(over, ("node", "local"), next_node(0))
    cross = lax.ppermute(cross, ("node", "local"), next_node(1))
    codes = lax.all_to_all(code(own, other, rows), "node", split_axis=0, concat_axis=0, tiled=True)
    table_new, accum_new = update(place, codes, over, cross, table, accum.reshape(32, 128))
    return table_new, accum_new.reshape(4096)


def solution(mesh):
    return jax.shard_map(
        per_device,
        mesh=mesh,
        in_specs=(
            P(("node", "local"), None),
            P(("node", "local")),
            P(("node", "local"), None),
            P(("node", "local")),
            P(("node", "local"), None),
            P(("node", "local")),
        ),
        out_specs=(P(("node", "local"), None), P(("node", "local"))),
        check_vma=False,
    )
```

```python
import jax
import jax.numpy as jnp
from jax import lax
from jax.experimental import pallas as pl
from jax.experimental.pallas import tpu as pltpu
from jax.sharding import PartitionSpec as P

LEARN_RATE = 0.3
EPSILON = 1e-06

LANES = 128
KEEP = 32
GROUP = 8
BLOCKS = 17
WIDTH = BLOCKS * LANES
BUCKET_ROWS = 40
F32, BF16, I32 = jnp.float32, jnp.bfloat16, jnp.int32


def rows_iota(rows, cols):
    return lax.broadcasted_iota(I32, (rows, cols), 0)


def lanes_iota(rows, cols):
    return lax.broadcasted_iota(I32, (rows, cols), 1)


def prep_kernel(slot_ref, len_ref, pooled_ref, out_ref, perm_ref):
    slot = slot_ref[...]
    present = rows_iota(*slot.shape) < len_ref[...]
    side = (slot >> 11) & 1
    owner = (slot >> 6) & 31
    place = slot & 63
    first = place < KEEP
    low = jnp.where(first, (owner & 3) * KEEP + place, side * KEEP + place - KEEP)
    block = (slot >> 12) * BLOCKS + jnp.where(first, side * 8 + (owner >> 2), 16)

    def by_group(x):
        parts = [x[:, LANES * b : LANES * (b + 1)] for b in range(4)]
        return jnp.concatenate(parts, axis=0).T.astype(BF16)

    mark = (1.0 + low.astype(F32) * (1.0 / 128.0)) * jnp.exp2((block - 34).astype(F32))
    out_ref[512:640, :] = by_group(jnp.where(present, mark, 0.0))
    for h in range(2):
        for b in range(4):
            start = b * 128 + h * 64
            perm_ref[pl.ds(h * 4 + b, 64, stride=GROUP), :] = pooled_ref[start : start + 64, :].astype(F32)
    for t in range(4):
        out_ref[t * 128 : (t + 1) * 128, :] = perm_ref[t * 128 : (t + 1) * 128, :].T.astype(BF16)


def add_sums(place_ref, piece, low_ref, code_ref, counts_ref):
    chip, core = place_ref[0], place_ref[1]
    span = jnp.where(chip == 0, 2.0**34, jnp.where(chip == 1, 2.0**17, jnp.where(chip == 2, 1.0, 2.0**-17))).astype(F32)
    mark = piece(512, 640).astype(F32) * span
    valid = (mark >= 1.0) & (mark < 2.0**BLOCKS)
    power = jnp.floor(jnp.log2(jnp.maximum(mark, 0.5)) + 0.002)
    low_ref[...] = jnp.round((mark * jnp.exp2(-power) - 1.0) * 128.0)
    block = jnp.clip(power, 0.0, 16.0).astype(I32)
    block = jnp.where(block < 16, block ^ (core * 8), block)
    member = (rows_iota(128, 128) >> 6) * 4 + (lanes_iota(128, 128) >> 5)
    code_ref[...] = jnp.where(valid, block * GROUP + member, -1).astype(F32)

    tiles = [(rows_iota(16, 128) + 16 * t).astype(F32).astype(BF16) for t in range(9)]
    one, zero = jnp.ones((16, 128), BF16), jnp.zeros((16, 128), BF16)

    def onehot(ref, row, count):
        halves = []
        for h in range(2):
            line = ref[pl.ds(row + h * 64, 1), :]
            line = jnp.broadcast_to(line, (16, 128)).astype(BF16)
            halves.append(jnp.concatenate([jnp.where(line == tiles[t], one, zero) for t in range(count)], axis=0))
        return jnp.concatenate(halves, axis=1).astype(jnp.float8_e4m3fn)

    def group_counts(row):
        return lax.dot_general(
            onehot(code_ref, row, 9), onehot(low_ref, row, 8), (((1,), (1,)), ((), ())), preferred_element_type=F32
        )

    def step(i, carry):
        first, second = group_counts(i * 2), group_counts(i * 2 + 1)
        at = pl.multiple_of(i * 16, 16)
        for b in range(BLOCKS):
            both = jnp.concatenate([first[b * 8 : b * 8 + 8, :], second[b * 8 : b * 8 + 8, :]], axis=0)
            counts_ref[pl.ds(at, 16), b * 128 : (b + 1) * 128] = both.astype(BF16)
        return carry

    lax.fori_loop(0, 32, step, 0, unroll=32)
    pooled = jnp.concatenate([piece(t * 128, t * 128 + 128) for t in range(4)], axis=1)
    return jnp.dot(pooled, counts_ref[...], preferred_element_type=F32)


def rows_of(ref):
    return lambda a, b: ref[a:b, :]


def own_kernel(place_ref, mine_ref, total_ref, low_ref, code_ref, counts_ref):
    total_ref[...] = add_sums(place_ref, rows_of(mine_ref), low_ref, code_ref, counts_ref)


def near_kernel(place_ref, near_ref, before_ref, total_ref, low_ref, code_ref, counts_ref):
    total_ref[...] = before_ref[...] + add_sums(place_ref, rows_of(near_ref), low_ref, code_ref, counts_ref)


def far_kernel(place_ref, far_ref, before_ref, row_ref, own_ref, other_ref, over_ref, cross_ref, low_ref, code_ref, counts_ref):
    total = before_ref[...] + add_sums(place_ref, rows_of(far_ref), low_ref, code_ref, counts_ref)
    own_ref[...] = total[:, :1024]
    other_ref[...] = total[:, 1024:2048]
    over = total[:, 2048:].T
    near = jnp.broadcast_to(place_ref[1] == 0, (KEEP, LANES))
    over_ref[0:32, :] = jnp.where(near, over[0:32, :], over[32:64, :])
    cross_ref[...] = jnp.where(near, over[32:64, :], over[0:32, :])
    line = row_ref[pl.ds(((place_ref[2] + 1) & 31) >> 1, 1), :] & 4095
    over_ref[32:40, :] = jnp.broadcast_to(line, (8, 128)).astype(F32)


def code_kernel(own_ref, got_ref, row_ref, out_ref):
    rows = row_ref[...] & 4095

    def coded(b):
        total = own_ref[:, b * 128 : (b + 1) * 128] + got_ref[:, b * 128 : (b + 1) * 128]
        most = jnp.max(jnp.abs(total), axis=0, keepdims=True)
        power = jnp.floor(jnp.log2(jnp.maximum(most, 1e-30))) + 1.0
        scaled = jnp.clip(jnp.round(total * jnp.exp2(15.0 - power)), -32767.0, 32767.0)
        return scaled.T.astype(I32).astype(jnp.int16), power.astype(I32)

    def tail(row_line, power_line):
        at = rows_iota(8, 128)
        out = jnp.where(at == 0, jnp.broadcast_to(row_line, (8, 128)), jnp.broadcast_to(power_line, (8, 128)))
        return out

    for b in range(8):
        codes, power = coded(b)
        for q in range(4):
            n = b * 4 + q
            out_ref[n, 0:32, :] = codes[q * 32 : (q + 1) * 32, :]
            out_ref[n, 32:40, :] = tail(rows[n >> 1 : (n >> 1) + 1, :], power).astype(jnp.int16)

def update_kernel(place_ref, got_ref, over_ref, cross_ref, table_ref, accum_ref, table_out, accum_out, value_ref, line_ref, fresh_ref, sems):
    node = place_ref[2]

    def halves(x):
        x = x.astype(I32)
        return (x >> 8).astype(F32).astype(BF16), (x & 255).astype(F32).astype(BF16)

    for m in range(32):
        high, low = halves(got_ref[m, 0:32, :])
        value_ref[m * 32 : (m + 1) * 32, 0:128] = high
        value_ref[m * 32 : (m + 1) * 32, 128:256] = low
    over = over_ref[0:32, :] + cross_ref[...]
    high = (over * (1.0 / 256.0)).astype(BF16)
    rest = over - high.astype(F32) * 256.0
    middle = rest.astype(BF16)
    value_ref[1024:1056, 0:128] = high
    value_ref[1024:1056, 128:256] = middle
    value_ref[1056:1088, 0:128] = jnp.zeros((32, 128), BF16)
    value_ref[1056:1088, 128:256] = (rest - middle.astype(F32)).astype(BF16)
    value_ref[1088:1152, :] = jnp.zeros((64, 256), BF16)

    quarter = lanes_iota(8, 128) >> 5
    ids, powers = jnp.zeros((8, 128), I32), jnp.zeros((8, 128), I32)
    for r in range(4):
        tails = [got_ref[kb * 4 + r, 32:40, :].astype(I32) for kb in range(8)]
        id_lines = jnp.concatenate([t[0:1, :] for t in tails], axis=0)
        power_lines = jnp.concatenate([t[1:2, :] for t in tails], axis=0)
        id_lines = pltpu.roll(id_lines, (r * 32 + 128 - (node & 1) * 64) & 127, axis=1)
        power_lines = pltpu.roll(power_lines, (r * 32 + 128 - (node & 3) * 32) & 127, axis=1)
        ids = jnp.where(quarter == r, id_lines, ids)
        powers = jnp.where(quarter == r, power_lines, powers)
    line_ref[0:8, :] = ids
    line_ref[8:16, :] = powers
    over_line = over_ref[32:40, :].astype(I32)
    first = pltpu.roll(over_line, (128 - ((node & 1) * 64 + 32)) & 127, axis=1)
    second = pltpu.roll(over_line, (128 - (node & 1) * 64) & 127, axis=1)
    lane = lanes_iota(8, 128)
    line_ref[16:24, :] = jnp.where(lane < 32, first, jnp.where(lane < 64, second, -1))

    tiles = [(rows_iota(16, 128) + 16 * t).astype(F32).astype(BF16) for t in range(16)]
    zero = jnp.zeros((16, 128), BF16)
    diag = rows_iota(128, 128) == lanes_iota(128, 128)
    scales = []
    for kb in range(9):
        scale = jnp.ones((1, 128), F32) if kb == 8 else jnp.exp2(line_ref[kb + 8 : kb + 9, :].astype(F32) - 15.0)
        scales.append(jnp.broadcast_to(scale, (16, 128)).astype(BF16))
    values = value_ref[...]

    copies = []
    for p in range(16):
        first_row = p * 256
        parts = []
        for kb in range(9):
            at_id = kb if kb < 8 else 16
            ids = (line_ref[at_id : at_id + 1, :] - first_row).astype(F32)
            ids = jnp.broadcast_to(ids, (16, 128)).astype(BF16)
            parts.append(jnp.concatenate([jnp.where(ids == tiles[t], scales[kb], zero) for t in range(16)], axis=0))
        hot = jnp.concatenate(parts, axis=1)
        both = jnp.dot(hot, values, preferred_element_type=F32)
        gradient = both[:, 0:128] * 256.0 + both[:, 128:256]
        for t in range(2):
            g = gradient[t * 128 : (t + 1) * 128, :]
            line = slice(p * 2 + t, p * 2 + t + 1)
            accum = jnp.broadcast_to(accum_ref[line, :], (128, 128))
            fresh = jnp.sum(g * g * (1.0 / 128.0) + jnp.where(diag, accum, 0.0), axis=1, keepdims=True)
            accum_out[line, :] = jnp.sum(jnp.where(diag, fresh, 0.0), axis=0, keepdims=True)
            step = g * (LEARN_RATE / (jnp.sqrt(fresh) + EPSILON))
            at = slice(p * 256 + t * 128, p * 256 + t * 128 + 128)
            fresh_ref[at, :] = table_ref[at, :] - step
        if p in (9, 13, 15):
            first = {9: 0, 13: 10, 15: 14}[p]
            done = pl.ds(first * 256, (p + 1 - first) * 256)
            copies.append(pltpu.make_async_copy(fresh_ref.at[done, :], table_out.at[done, :], sems.at[len(copies)]))
            copies[-1].start()
    for copy in copies:
        copy.wait()


VMEM = pl.BlockSpec(memory_space=pltpu.VMEM)
SMEM = pl.BlockSpec(memory_space=pltpu.SMEM)
PARAMS = pltpu.CompilerParams(vmem_limit_bytes=40 * 1024 * 1024)


def whole(*shape):
    return pl.BlockSpec(shape, lambda i: (0,) * len(shape))


def prep(slot_t, lengths, pooled):
    return pl.pallas_call(
        prep_kernel,
        grid=(1,),
        out_shape=jax.ShapeDtypeStruct((640, 128), BF16),
        in_specs=[whole(32, 512), whole(1, 512), whole(512, 128)],
        out_specs=VMEM,
        scratch_shapes=[pltpu.VMEM((512, 128), F32)],
        compiler_params=pltpu.CompilerParams(vmem_limit_bytes=63 * 1024 * 1024),
        name="prep",
    )(slot_t, lengths, pooled)


def sums_call(kernel, name, outs, *args):
    return pl.pallas_call(
        kernel,
        out_shape=[jax.ShapeDtypeStruct(shape, F32) for shape in outs],
        in_specs=[SMEM] + [VMEM] * (len(args) - 1),
        out_specs=[VMEM] * len(outs),
        scratch_shapes=[pltpu.VMEM((128, 128), F32), pltpu.VMEM((128, 128), F32), pltpu.VMEM((512, WIDTH), BF16)],
        compiler_params=PARAMS,
        cost_estimate=pl.CostEstimate(flops=2_000_000_000, bytes_accessed=3_000_000, transcendentals=0),
        name=name,
    )(*args)


def gather_sums(place, packed, rows):
    shift = lambda x, k: lax.ppermute(x, "local", [(i, (i + k) % 8) for i in range(8)])
    left, right = shift(packed, 2), shift(packed, 6)
    (total,) = sums_call(own_kernel, "own_sums", [(128, WIDTH)], place, packed)
    packed, total = lax.optimization_barrier((packed, total))
    far = shift(packed, 4)
    left, total = lax.optimization_barrier((left, total))
    (total,) = sums_call(near_kernel, "left_sums", [(128, WIDTH)], place, left, total)
    right, total = lax.optimization_barrier((right, total))
    (total,) = sums_call(near_kernel, "right_sums", [(128, WIDTH)], place, right, total)
    outs = [(128, 1024), (128, 1024), (40, 128), (32, 128)]
    return sums_call(far_kernel, "far_sums", outs, place, far, total, rows)


def code(own, got, slot_row):
    return pl.pallas_call(
        code_kernel,
        out_shape=jax.ShapeDtypeStruct((32, BUCKET_ROWS, 128), jnp.int16),
        in_specs=[VMEM] * 3,
        out_specs=VMEM,
        compiler_params=PARAMS,
        name="code",
    )(own, got, slot_row)


def update(place, got, over, cross, table, accum):
    return pl.pallas_call(
        update_kernel,
        out_shape=[jax.ShapeDtypeStruct((4096, 128), F32), jax.ShapeDtypeStruct((32, 128), F32)],
        in_specs=[SMEM] + [VMEM] * 5,
        out_specs=[pl.BlockSpec(memory_space=pl.ANY), VMEM],
        scratch_shapes=[
            pltpu.VMEM((1152, 256), BF16),
            pltpu.VMEM((24, 128), I32),
            pltpu.VMEM((4096, 128), F32),
            pltpu.SemaphoreType.DMA((3,)),
        ],
        compiler_params=PARAMS,
        name="update",
    )(place, got, over, cross, table, accum)


def next_node(flip):
    return [(n * 8 + i, (n + 1) % 32 * 8 + (i ^ flip)) for n in range(32) for i in range(8)]


def per_device(pooled_grad, lengths, slot_of, slot_row, table, accum):
    local, node = lax.axis_index("local"), lax.axis_index("node")
    place = jnp.stack([local >> 1, local & 1, node]).astype(I32)
    packed = prep(slot_of.T, lengths.reshape(1, 512), pooled_grad)
    rows = slot_row.reshape(16, 128)
    own, other, over, cross = gather_sums(place, packed, rows)
    other = lax.ppermute(other, "local", [(i, i ^ 1) for i in range(8)])
    over = lax.ppermute(over, ("node", "local"), next_node(0))
    cross = lax.ppermute(cross, ("node", "local"), next_node(1))
    codes = lax.all_to_all(code(own, other, rows), "node", split_axis=0, concat_axis=0, tiled=True)
    table_new, accum_new = update(place, codes, over, cross, table, accum.reshape(32, 128))
    return table_new, accum_new.reshape(4096)


def solution(mesh):
    return jax.shard_map(
        per_device,
        mesh=mesh,
        in_specs=(
            P(("node", "local"), None),
            P(("node", "local")),
            P(("node", "local"), None),
            P(("node", "local")),
            P(("node", "local"), None),
            P(("node", "local")),
        ),
        out_specs=(P(("node", "local"), None), P(("node", "local"))),
        check_vma=False,
    )
```
